128 devices in a mesh: gx: 16 (over z, y), gy: 8 (over x, core).
Axes of the slice: x: 4, y: 4, z: 4, core: 2. Of those that a mesh axis runs over, the one named last changes fastest.
Arguments:
- tiles: float32 [16, 8, 2, 40, 40, 128], P('gx', 'gy'), may hold values from 0.25 to 4
- shifts: int32 [16, 8, 2], P('gx', 'gy'), may hold values from -4 to 4
- extents: int32 [16, 8, 4], P('gx', 'gy'), may hold values from 4 to 12
- conv1_weight: bfloat16 [3, 3, 3, 2, 32], replicated, may hold values from -0.875 to 0.875
- conv1_bias: float32 [32], replicated, may hold values from -3 to 3
- conv2_weight: bfloat16 [3, 3, 3, 32, 32], replicated, may hold values from -0.21875 to 0.21875
- conv2_bias: float32 [32], replicated, may hold values from -3 to 3
- head_weight: bfloat16 [32, 2], replicated, may hold values from -1 to 1
- head_bias: float32 [2], replicated, may hold values from -3 to 3
Outputs:
- joined: float32 [2, 256, 128, 128], P(None, 'gx', 'gy')
- restored: float32 [2, 256, 128, 128], P(None, 'gx', 'gy')
The draws below stay inside these ranges and needn't reach their ends.
All inputs are finite; a program needn't handle non-finite values.
Results may differ from the reference program's by a relative error of at most 0.0057.
Values may be sent and summed in bfloat16 or wider, within the bound.
A program may use at most 64 MiB of HBM per device.

```python
import math
import jax
import jax.numpy as jnp
from jax import lax

CHANNELS = 2
FEATURES = 32
ROWS_DEV = 16
COLS_DEV = 16
DEPTH = 128
MARGIN = 12
SHIFT = 4
RAMP = 8
TILE_ROWS = 16
TILE_COLS = 8
ROWS = 256
COLS = 128
TILE_HEIGHT = 40
TILE_WIDTH = 40


def with_ends(result, own_key, smallest, largest):
    extent = result.shape
    index_at = [jax.random.randint(jax.random.fold_in(own_key, axis), (), 0, extent[axis]) for axis in range(len(extent))]
    result = result.at[tuple(index_at)].set(smallest)
    longest = extent.index(max(extent))
    index_at[longest] = (index_at[longest] + 1) % extent[longest]
    return result.at[tuple(index_at)].set(largest)


def block_scale(own_key, shape, cuts, low, top_value):
    level, own = 1.0, jax.random.fold_in(own_key, 6)
    for position, shards_of in cuts:
        steps = jnp.exp(jax.random.uniform(jax.random.fold_in(own, position), (shards_of,), jnp.float32, low / len(cuts), top_value / len(cuts)))
        level = level * jnp.repeat(steps, shape[position] // shards_of).reshape([-1 if axis == position else 1 for axis in range(len(shape))])
    return level


def scatter_about(stream_key, dims, width, most, kind=jnp.bfloat16):
    array = jax.random.normal(stream_key, dims, jnp.float32) * width
    return jnp.minimum(jnp.maximum(array, -most), most).astype(kind)


def setup_inputs(seed: int = 0) -> dict:
    seeds = jax.random.split(jax.random.key(seed), 10)
    return {
        "tiles": jnp.clip(jnp.exp(math.log(4.0) - 2.7725887 * jax.random.uniform(seeds[0], (TILE_ROWS, TILE_COLS, CHANNELS, TILE_HEIGHT, TILE_WIDTH, DEPTH), jnp.float32) ** block_scale(seeds[0], (TILE_ROWS, TILE_COLS, CHANNELS, TILE_HEIGHT, TILE_WIDTH, DEPTH), ((0, 16), (1, 8)), -0.2, 0.2)), 0.25, 4.0),
        "shifts": with_ends(jax.random.randint(seeds[1], (TILE_ROWS, TILE_COLS, 2), 0 - SHIFT, SHIFT + 1), jax.random.fold_in(seeds[1], 1), 0 - SHIFT, SHIFT).astype(jnp.int32),
        "extents": with_ends(jax.random.randint(seeds[2], (TILE_ROWS, TILE_COLS, 4), SHIFT, MARGIN + 1), jax.random.fold_in(seeds[2], 1), SHIFT, MARGIN).astype(jnp.int32),
        "conv1_weight": scatter_about(seeds[3], (3, 3, 3, CHANNELS, FEATURES), (27 * CHANNELS) ** -0.5, 0.875),
        "conv1_bias": scatter_about(seeds[4], (FEATURES,), 0.5, 3.0, jnp.float32),
        "conv2_weight": scatter_about(seeds[5], (3, 3, 3, FEATURES, FEATURES), (27 * FEATURES) ** -0.5, 0.21875),
        "conv2_bias": scatter_about(seeds[6], (FEATURES,), 0.5, 3.0, jnp.float32),
        "head_weight": scatter_about(seeds[7], (FEATURES, CHANNELS), FEATURES ** -0.5, 1.0),
        "head_bias": scatter_about(seeds[8], (CHANNELS,), 0.5, 3.0, jnp.float32),
    }


def feather(low, high, length):
    places = jnp.arange(length, dtype=jnp.int32)
    inside = (places >= low) & (places < high)
    ramped = jnp.minimum(jnp.minimum(places - low + 1, high - places), RAMP)
    return jnp.where(inside, ramped.astype(jnp.float32), jnp.float32(0.0)) / RAMP


def conv_valid(source, weight):
    kernel = jnp.transpose(weight.astype(jnp.float32), (4, 3, 0, 1, 2))
    return lax.conv_general_dilated(source[None], kernel, (1, 1, 1), "VALID", precision=lax.Precision.HIGHEST)[0]


def reference(tiles, shifts, extents, conv1_weight, conv1_bias, conv2_weight, conv2_bias, head_weight, head_bias):
    rim_width = MARGIN + SHIFT
    canvas_sum = jnp.zeros((CHANNELS, ROWS + 2 * rim_width, COLS + 2 * rim_width, DEPTH), jnp.float32)
    canvas_wts = jnp.zeros((ROWS + 2 * rim_width, COLS + 2 * rim_width), jnp.float32)

    def add_tile(tile_index, carry):
        canvas_sum, canvas_wts = carry
        tile_index = jnp.asarray(tile_index).astype(jnp.int32)
        tile_row = tile_index // TILE_COLS
        tile_col = tile_index % TILE_COLS
        own_tile = tiles[tile_row, tile_col]
        offsets = shifts[tile_row, tile_col]
        margins = extents[tile_row, tile_col]
        weight = feather(MARGIN - margins[0], MARGIN + ROWS_DEV + margins[1], TILE_HEIGHT)[:, None] * feather(MARGIN - margins[2], MARGIN + COLS_DEV + margins[3], TILE_WIDTH)[None, :]
        top_row = tile_row * ROWS_DEV + SHIFT + offsets[0]
        left_col = tile_col * COLS_DEV + SHIFT + offsets[1]
        zero_index = jnp.int32(0)
        block_sum = lax.dynamic_slice(canvas_sum, (zero_index, top_row, left_col, zero_index), (CHANNELS, TILE_HEIGHT, TILE_WIDTH, DEPTH)) + own_tile * weight[None, :, :, None]
        canvas_sum = lax.dynamic_update_slice(canvas_sum, block_sum, (zero_index, top_row, left_col, zero_index))
        block_wts = lax.dynamic_slice(canvas_wts, (top_row, left_col), (TILE_HEIGHT, TILE_WIDTH)) + weight
        canvas_wts = lax.dynamic_update_slice(canvas_wts, block_wts, (top_row, left_col))
        return canvas_sum, canvas_wts

    canvas_sum, canvas_wts = lax.fori_loop(0, TILE_ROWS * TILE_COLS, add_tile, (canvas_sum, canvas_wts))
    joined = canvas_sum[:, rim_width:rim_width + ROWS, rim_width:rim_width + COLS] / canvas_wts[rim_width:rim_width + ROWS, rim_width:rim_width + COLS][None, :, :, None]
    low_image = joined.astype(jnp.bfloat16).astype(jnp.float32)
    padded = jnp.pad(low_image, ((0, 0), (2, 2), (1, 1), (1, 1)))

    def one_block(block_index):
        first_row = block_index.astype(jnp.int32) * ROWS_DEV
        zero_index = jnp.int32(0)
        window = lax.dynamic_slice(padded, (zero_index, first_row, zero_index, zero_index), (CHANNELS, ROWS_DEV + 4, COLS + 2, DEPTH + 2))
        first_act = jax.nn.relu(conv_valid(window, conv1_weight) + conv1_bias[:, None, None, None])
        row_ids = first_row - 1 + jnp.arange(ROWS_DEV + 2, dtype=jnp.int32)
        keep = (row_ids >= 0) & (row_ids < ROWS)
        first_act = jnp.where(keep[None, :, None, None], first_act, 0.0).astype(jnp.bfloat16).astype(jnp.float32)
        first_act = jnp.pad(first_act, ((0, 0), (0, 0), (1, 1), (1, 1)))
        second = jax.nn.relu(conv_valid(first_act, conv2_weight) + conv2_bias[:, None, None, None])
        second = second.astype(jnp.bfloat16).astype(jnp.float32)
        projected = jnp.einsum("oc,orxz->crxz", head_weight.astype(jnp.float32), second, precision=lax.Precision.HIGHEST)
        return projected + head_bias[:, None, None, None]

    blocks = lax.map(one_block, jnp.arange(TILE_ROWS, dtype=jnp.int32))
    restored = jnp.transpose(blocks, (1, 0, 2, 3, 4)).reshape(CHANNELS, ROWS, COLS, DEPTH)
    return joined, restored
```

```python
import jax
import jax.numpy as jnp
from jax import lax
from jax.experimental import pallas as pl
from jax.experimental.pallas import tpu as pltpu
from jax.sharding import PartitionSpec as P

MESH = pl.DeviceIdType.MESH
F32 = jnp.float32
BF16 = jnp.bfloat16
I16 = jnp.int16
STEP_Y = 4.0 / 32767
STEP_X = 12.0 / 32767
PAD = 8
CHUNKS = (32, 0, 40, 8, 16, 24)


def ramp(places, before, after):
    rise = places + 1.0 + before
    fall = 16.0 + after - places
    return jnp.clip(jnp.minimum(rise, fall), 0.0, 8.0) * 0.125


def code(values, step):
    return jnp.round(values * (1.0 / step)).astype(jnp.int32).astype(I16)


def decode(values, step):
    return values.astype(jnp.int32).astype(F32) * step


def when(condition, action):
    pl.when(condition)(action)


def iota(shape, dim):
    return lax.broadcasted_iota(jnp.int32, shape, dim).astype(F32)


def kernel(
    nx, ny,
    tiles, shifts, extents, w1, b1, w2, b2, hw, hb,
    joined, restored,
    tile, sides, landed, metas, metas_x, across, landed_x, image, stack1, first,
    w1_in, w2_in, hw_in, band1, band2, head, bias1, bias2, flat1,
    in_sem, send_y, recv_y, send_x, recv_x, send_m, recv_m, send_h, recv_h,
):
    p, q = lax.axis_index("gx"), lax.axis_index("gy")
    up, down = lax.rem(p + nx - 1, nx), lax.rem(p + 1, nx)
    left, right = lax.rem(q + ny - 1, ny), lax.rem(q + 1, ny)

    load = pltpu.make_async_copy(tiles.at[0, 0], tile.at[:, PAD:PAD + 40, PAD:PAD + 40], in_sem.at[0])
    load.start()
    loads = [
        pltpu.make_async_copy(w1, w1_in, in_sem.at[1]),
        pltpu.make_async_copy(w2, w2_in, in_sem.at[2]),
        pltpu.make_async_copy(hw, hw_in, in_sem.at[3]),
    ]
    for one in loads:
        one.start()
    barrier = pltpu.get_barrier_semaphore()
    is_up, is_down, is_left, is_right = p > 0, p < nx - 1, q > 0, q < ny - 1
    near = ((is_left, (p, left)), (is_right, (p, right)), (is_up, (up, q)), (is_down, (down, q)))
    for there_is, there in near:
        @pl.when(there_is)
        def _():
            pl.semaphore_signal(barrier, inc=1, device_id=there, device_id_type=MESH)

    @pl.when(q == 0)
    def _():
        landed[1] = jnp.zeros((2, 48, 16, 128), I16)
        metas_x[0, 1] = jnp.full((8, 128), -100.0, F32)
        image[:, :, 6:8] = jnp.zeros((2, 20, 2, 128), F32)

    @pl.when(q == ny - 1)
    def _():
        landed[0] = jnp.zeros((2, 48, 16, 128), I16)
        metas_x[0, 2] = jnp.full((8, 128), -100.0, F32)
        image[:, :, 24:26] = jnp.zeros((2, 20, 2, 128), F32)

    @pl.when(p == 0)
    def _():
        landed_x[1] = jnp.zeros((2, 16, 16, 128), I16)
        metas_x[1] = jnp.full((3, 8, 128), -100.0, F32)
        image[:, 0:2] = jnp.zeros((2, 2, 32, 128), F32)

    @pl.when(p == nx - 1)
    def _():
        landed_x[0] = jnp.zeros((2, 16, 16, 128), I16)
        metas_x[2] = jnp.full((3, 8, 128), -100.0, F32)
        image[:, 18:20] = jnp.zeros((2, 2, 32, 128), F32)

    tile[:, 0:PAD] = jnp.zeros((2, PAD, 56, 128), F32)
    tile[:, 48:56] = jnp.zeros((2, PAD, 56, 128), F32)
    tile[:, PAD:48, 0:PAD] = jnp.zeros((2, 40, PAD, 128), F32)
    tile[:, PAD:48, 48:56] = jnp.zeros((2, 40, PAD, 128), F32)

    s0, s1 = shifts[0, 0, 0], shifts[0, 0, 1]
    values = [shifts[0, 0, 0], shifts[0, 0, 1]] + [extents[0, 0, k] for k in range(4)]
    values = [v.astype(F32) for v in values]
    s0f, s1f, m0, m1, m2, m3 = values
    for k in range(6):
        metas[0, k:k + 1] = jnp.full((1, 128), values[k], F32)

    near_count = sum(there_is.astype(jnp.int32) for there_is, _ in near)
    pl.semaphore_wait(barrier, near_count)
    meta_copies = [
        pltpu.make_async_remote_copy(metas.at[0], metas_x.at[0, 2], send_m.at[0], recv_m.at[0],
                                     device_id=(p, left), device_id_type=MESH),
        pltpu.make_async_remote_copy(metas.at[0], metas_x.at[0, 1], send_m.at[1], recv_m.at[1],
                                     device_id=(p, right), device_id_type=MESH),
    ]
    when(is_left, meta_copies[0].start)
    when(is_right, meta_copies[1].start)
    load.wait()

    def own(r0, c0, width_vec):
        rows = ramp(iota((8, 1, 128), 0) + (r0 - 16.0) - s0f, m0, m1)
        weight = rows * width_vec
        return tile[:, pl.ds(r0 + 4 - s0 , 8), pl.ds(c0 + 4 - s1, 16), :] * weight[None]

    def columns(c0):
        return ramp(iota((1, 16, 128), 1) + (c0 - 16.0) - s1f, m2, m3)

    col_left, col_mid, col_right = columns(0), columns(16), columns(32)
    copies_y = []
    for k, r0 in enumerate(CHUNKS):
        for side, (c0, vec, there) in enumerate(((0, col_left, left), (32, col_right, right))):
            sides[side, :, r0:r0 + 8] = code(own(r0, c0, vec), STEP_Y)
            one = pltpu.make_async_remote_copy(
                sides.at[side, :, r0:r0 + 8], landed.at[side, :, r0:r0 + 8],
                send_y.at[side, k], recv_y.at[side, k], device_id=(p, there), device_id_type=MESH)
            when(is_right if side else is_left, one.start)
            copies_y.append(one)

    when(is_right, meta_copies[0].wait_recv)
    when(is_left, meta_copies[1].wait_recv)
    metas_x[0, 0] = metas[0]
    copies_m = [
        pltpu.make_async_remote_copy(metas_x.at[0], metas_x.at[2], send_m.at[2], recv_m.at[2],
                                     device_id=(up, q), device_id_type=MESH),
        pltpu.make_async_remote_copy(metas_x.at[0], metas_x.at[1], send_m.at[3], recv_m.at[3],
                                     device_id=(down, q), device_id_type=MESH),
    ]
    when(is_up, copies_m[0].start)
    when(is_down, copies_m[1].start)

    copies_x = []
    for k in range(4):
        r0 = CHUNKS[k]
        when(is_right, copies_y[2 * k].wait_recv)
        when(is_left, copies_y[2 * k + 1].wait_recv)
        side = 1 if r0 >= 32 else 0
        at = r0 - 32 if r0 >= 32 else r0
        total = own(r0, 16, col_mid)
        total = total + decode(landed[0, :, r0:r0 + 8], STEP_Y) + decode(landed[1, :, r0:r0 + 8], STEP_Y)
        across[side, :, at:at + 8] = code(total, STEP_X)
        one = pltpu.make_async_remote_copy(
            across.at[side, :, at:at + 8], landed_x.at[side, :, at:at + 8],
            send_x.at[k], recv_x.at[k], device_id=(down if side else up, q), device_id_type=MESH)
        when(is_down if side else is_up, one.start)
        copies_x.append(one)

    for one in loads:
        one.wait()
    bias1[...] = jnp.zeros((32, 128), F32)
    for k in range(32):
        bias1[k:k + 1] = jnp.full((1, 128), b1[k], F32)
        bias2[k:k + 1] = jnp.full((1, 128), b2[k], F32)
    flat1[...] = jnp.zeros((64, 32), F32)
    for dr in range(3):
        for dc in range(3):
            for dz in range(3):
                at = ((dz * 3 + dr) * 3 + dc) * 2
                flat1[at:at + 2] = w1_in[dr, dc, dz].astype(F32)
    tap = lax.broadcasted_iota(jnp.int32, (64, 256), 0)
    lane = lax.broadcasted_iota(jnp.int32, (64, 256), 1)
    target = (tap // 18) * 80 + ((tap // 6) % 3) * 16 + (tap % 2) * 8 + (tap // 2) % 3
    spread = jnp.where((lane == target) & (tap < 54), 1.0, 0.0).astype(BF16)
    strip = lax.dot_general(flat1[...].astype(BF16), spread, (((0,), (0,)), ((), ())),
                            preferred_element_type=F32)
    for orow in range(3):
        for ocol in range(6):
            at = (orow * 6 + ocol) * 32
            band1[at:at + 32] = pltpu.roll(strip, orow * 16 + ocol, 1).astype(BF16)
    zero = jnp.zeros((32, 128), BF16)
    for dz in range(3):
        strips = []
        for dr in range(3):
            taps = jnp.concatenate(
                [w2_in[dr, dc, dz].astype(F32) for dc in range(3)] + [jnp.zeros((32, 32), F32)], axis=0)
            taps = jnp.concatenate([taps, jnp.zeros((128, 96), F32)], axis=1)
            flipped = taps.T[0:32]
            strips.append((flipped.astype(BF16), pltpu.roll(flipped, 32, 1).astype(BF16)))
        for orow in range(2):
            for ocol in range(2):
                at = dz * 128 + (orow * 2 + ocol) * 32
                for irow in range(4):
                    dr = irow - orow
                    band2[at:at + 32, irow * 128:irow * 128 + 128] = (
                        strips[dr][ocol] if 0 <= dr < 3 else zero)
    hrow = lax.broadcasted_iota(jnp.int32, (32, 512), 0)
    hlane = lax.broadcasted_iota(jnp.int32, (32, 512), 1)
    feat = lax.broadcasted_iota(jnp.int32, (32, 512), 0)
    pick = jnp.where(feat == hlane % 32, 1.0, 0.0).astype(BF16)
    per_lane = jnp.dot(hw_in[...], pick, preferred_element_type=F32)
    cell_row = (hlane // 64) % 2
    cell_col = (hlane // 128) * 2 + (hlane // 32) % 2
    match = ((hrow // 8) % 2 == cell_row) & (hrow % 8 == cell_col)
    by_channel = jnp.where(hrow < 16, per_lane[0:1], per_lane[1:2])
    head[...] = jnp.where(match, by_channel, 0.0).astype(BF16)

    when(is_down, copies_m[0].wait_recv)
    when(is_up, copies_m[1].wait_recv)
    for k in (4, 5):
        when(is_right, copies_y[2 * k].wait_recv)
        when(is_left, copies_y[2 * k + 1].wait_recv)
    for k, one in enumerate(copies_x):
        when(is_down if CHUNKS[k] < 32 else is_up, one.wait_recv)
    for r0 in (0, 8):
        total = own(16 + r0, 16, col_mid)
        total = total + decode(landed[0, :, 16 + r0:24 + r0], STEP_Y) + decode(landed[1, :, 16 + r0:24 + r0], STEP_Y)
        total = total + decode(landed_x[0, :, r0:r0 + 8], STEP_X) + decode(landed_x[1, :, r0:r0 + 8], STEP_X)
        weights = jnp.zeros((8, 16, 128), F32)
        for i, dp in ((0, 0), (1, -1), (2, 1)):
            for j, dq in ((0, 0), (1, -1), (2, 1)):
                meta = metas_x[i, j]
                at = [meta[k:k + 1][None] for k in range(6)]
                rows = ramp(iota((8, 1, 128), 0) + (r0 - 16.0 * dp) - at[0], at[2], at[3])
                cols = ramp(iota((1, 16, 128), 1) - 16.0 * dq - at[1], at[4], at[5])
                weights = weights + rows * cols
        cells = total / weights[None]
        joined[:, r0:r0 + 8] = cells
        image[:, 2 + r0:10 + r0, 8:24] = cells

    halo = [
        (is_up, is_down, (up, q), (slice(2, 4), slice(8, 24)), (slice(18, 20), slice(8, 24))),
        (is_down, is_up, (down, q), (slice(16, 18), slice(8, 24)), (slice(0, 2), slice(8, 24))),
        (is_left, is_right, (p, left), (slice(2, 18), slice(8, 10)), (slice(2, 18), slice(24, 26))),
        (is_right, is_left, (p, right), (slice(2, 18), slice(22, 24)), (slice(2, 18), slice(6, 8))),
        (is_up & is_left, is_down & is_right, (up, left), (slice(2, 4), slice(8, 10)), (slice(18, 20), slice(24, 26))),
        (is_up & is_right, is_down & is_left, (up, right), (slice(2, 4), slice(22, 24)), (slice(18, 20), slice(6, 8))),
        (is_down & is_left, is_up & is_right, (down, left), (slice(16, 18), slice(8, 10)), (slice(0, 2), slice(24, 26))),
        (is_down & is_right, is_up & is_left, (down, right), (slice(16, 18), slice(22, 24)), (slice(0, 2), slice(6, 8))),
    ]
    copies_h = []
    for k, (out, _, there, (rs, cs), (rd, cd)) in enumerate(halo):
        one = pltpu.make_async_remote_copy(
            image.at[:, rs, cs], image.at[:, rd, cd], send_h.at[k], recv_h.at[k],
            device_id=there, device_id_type=MESH)
        when(out, one.start)
        copies_h.append(one)
    for one, way in zip(copies_h, halo):
        when(way[1], one.wait_recv)

    plane = lax.broadcasted_iota(jnp.int32, (20, 16, 128), 2)
    for cb in range(3):
        at = 6 + 6 * cb
        cells = jnp.concatenate([image[0, :, at:at + 8], image[1, :, at:at + 8]], axis=1)
        stack1[cb, 1] = cells.astype(BF16)
        stack1[cb, 0] = jnp.where(plane == 0, 0.0, pltpu.roll(cells, 1, 2)).astype(BF16)
        stack1[cb, 2] = jnp.where(plane == 127, 0.0, pltpu.roll(cells, 127, 2)).astype(BF16)

    def conv1(step, carry):
        cb, rb = step // 3, step % 3
        halves = []
        for a in range(2):
            r0 = rb * 6 + a * 3
            parts = [stack1[cb, dz, pl.ds(r0, 5)].reshape(80, 128) for dz in range(3)]
            halves.append(jnp.concatenate(parts + [jnp.zeros((16, 128), BF16)], axis=0))
        out = jnp.dot(band1[...], jnp.concatenate(halves, axis=1), preferred_element_type=F32)
        bias = jnp.concatenate([bias1[...]] * 2, axis=1)
        out = jnp.maximum(out.reshape(18, 32, 256) + bias[None], 0.0).astype(BF16)
        out = out.reshape(3, 6, 32, 256)
        for a in range(2):
            first[pl.ds(rb * 6 + a * 3, 3), pl.ds(cb * 6, 6)] = out[:, :, :, a * 128:a * 128 + 128]
        return carry

    lax.fori_loop(0, 9, conv1, 0)

    @pl.when(p == 0)
    def _():
        first[0:1] = jnp.zeros((1, 18, 32, 128), BF16)

    @pl.when(p == nx - 1)
    def _():
        first[17:18] = jnp.zeros((1, 18, 32, 128), BF16)

    @pl.when(q == 0)
    def _():
        first[:, 0:1] = jnp.zeros((18, 1, 32, 128), BF16)

    @pl.when(q == ny - 1)
    def _():
        first[:, 17:18] = jnp.zeros((18, 1, 32, 128), BF16)

    def conv2(step, carry):
        quad, half = step // 2, step % 2
        lanes = lax.broadcasted_iota(jnp.int32, (128, 256), 1) % 128
        bias = jnp.concatenate([jnp.concatenate([bias2[...]] * 4, axis=0)] * 2, axis=1)
        seconds = []
        for b in range(4):
            c0 = half * 8 + 2 * b
            blocks = [first[pl.ds(quad * 4 + 2 * a, 4), pl.ds(c0, 4)].reshape(512, 128) for a in range(2)]
            out = jnp.dot(band2[...], jnp.concatenate(blocks, axis=1), preferred_element_type=F32)
            low, high = out[0:128], out[256:384]
            low = jnp.concatenate([pltpu.roll(low[:, 0:128], 1, 1), pltpu.roll(low[:, 128:256], 1, 1)], axis=1)
            high = jnp.concatenate([pltpu.roll(high[:, 0:128], 127, 1), pltpu.roll(high[:, 128:256], 127, 1)], axis=1)
            total = out[128:256] + jnp.where(lanes == 0, 0.0, low) + jnp.where(lanes == 127, 0.0, high)
            seconds.append(jnp.maximum(total + bias, 0.0).astype(BF16))
        out = jnp.dot(head[...], jnp.concatenate(seconds, axis=0), preferred_element_type=F32)
        for ch in range(2):
            for a in range(2):
                for r in range(2):
                    at = ch * 16 + r * 8
                    restored[ch, quad * 4 + 2 * a + r, pl.ds(half * 8, 8), :] = (
                        out[at:at + 8, a * 128:a * 128 + 128] + hb[ch])
        return carry

    lax.fori_loop(0, 8, conv2, 0)

    when(is_left, meta_copies[0].wait_send)
    when(is_right, meta_copies[1].wait_send)
    for k, one in enumerate(copies_y):
        when(is_right if k % 2 else is_left, one.wait_send)
    when(is_up, copies_m[0].wait_send)
    when(is_down, copies_m[1].wait_send)
    for k, one in enumerate(copies_x):
        when(is_down if CHUNKS[k] >= 32 else is_up, one.wait_send)
    for one, way in zip(copies_h, halo):
        when(way[0], one.wait_send)


def shards(tiles, shifts, extents, w1, b1, w2, b2, hw, hb):
    nx, ny = lax.axis_size("gx"), lax.axis_size("gy")
    vmem = pl.BlockSpec(memory_space=pltpu.VMEM)
    smem = pl.BlockSpec(memory_space=pltpu.SMEM)
    hbm = pl.BlockSpec(memory_space=pl.ANY)

    def body(*refs):
        kernel(nx, ny, *refs)

    dma = pltpu.SemaphoreType.DMA
    return pl.pallas_call(
        body,
        out_shape=[jax.ShapeDtypeStruct((2, 16, 16, 128), F32)] * 2,
        in_specs=[hbm, smem, smem, hbm, smem, hbm, smem, hbm, smem],
        out_specs=[vmem, vmem],
        scratch_shapes=[
            pltpu.VMEM((2, 56, 56, 128), F32),
            pltpu.VMEM((2, 2, 48, 16, 128), I16),
            pltpu.VMEM((2, 2, 48, 16, 128), I16),
            pltpu.VMEM((1, 8, 128), F32),
            pltpu.VMEM((3, 3, 8, 128), F32),
            pltpu.VMEM((2, 2, 16, 16, 128), I16),
            pltpu.VMEM((2, 2, 16, 16, 128), I16),
            pltpu.VMEM((2, 20, 32, 128), F32),
            pltpu.VMEM((3, 3, 20, 16, 128), BF16),
            pltpu.VMEM((18, 18, 32, 128), BF16),
            pltpu.VMEM((3, 3, 3, 2, 32), BF16),
            pltpu.VMEM((3, 3, 3, 32, 32), BF16),
            pltpu.VMEM((2, 32), BF16),
            pltpu.VMEM((576, 256), BF16),
            pltpu.VMEM((384, 512), BF16),
            pltpu.VMEM((32, 512), BF16),
            pltpu.VMEM((32, 128), F32),
            pltpu.VMEM((32, 128), F32),
            pltpu.VMEM((64, 32), F32),
            dma((4,)), dma((2, 6)), dma((2, 6)), dma((4,)), dma((4,)), dma((4,)), dma((4,)), dma((8,)), dma((8,)),
        ],
        compiler_params=pltpu.CompilerParams(
            collective_id=0, has_side_effects=True, vmem_limit_bytes=60 * 1024 * 1024),
    )(tiles, shifts, extents, w1, b1, w2, b2, hw.T, hb)


def solution(mesh):
    return jax.shard_map(
        shards,
        mesh=mesh,
        in_specs=(P("gx", "gy"), P("gx", "gy"), P("gx", "gy"), P(), P(), P(), P(), P(), P()),
        out_specs=(P(None, "gx", "gy", None), P(None, "gx", "gy", None)),
        check_vma=False,
    )
```

```python
import jax
import jax.numpy as jnp
from jax import lax
from jax.experimental import pallas as pl
from jax.experimental.pallas import tpu as pltpu
from jax.sharding import PartitionSpec as P

MESH = pl.DeviceIdType.MESH
F32 = jnp.float32
BF16 = jnp.bfloat16
I16 = jnp.int16
STEP_Y = 4.0 / 32767
STEP_X = 12.0 / 32767
PAD = 8
CHUNKS = (32, 0, 40, 8, 16, 24)


def ramp(places, before, after):
    rise = places + 1.0 + before
    fall = 16.0 + after - places
    return jnp.clip(jnp.minimum(rise, fall), 0.0, 8.0) * 0.125


def code(values, step):
    return jnp.round(values * (1.0 / step)).astype(jnp.int32).astype(I16)


def decode(values, step):
    return values.astype(jnp.int32).astype(F32) * step


def when(condition, action):
    pl.when(condition)(action)


def shift_planes(x, by):
    lane = lax.broadcasted_iota(jnp.int32, x.shape[:-1] + (128,), x.ndim - 1)
    parts = []
    for g in range(x.shape[-1] // 128):
        one = pltpu.roll(x[..., g * 128:g * 128 + 128], by % 128, x.ndim - 1)
        parts.append(jnp.where(lane == (0 if by > 0 else 127), 0.0, one))
    return jnp.concatenate(parts, axis=-1)


def iota(shape, dim):
    return lax.broadcasted_iota(jnp.int32, shape, dim).astype(F32)


def kernel(
    nx, ny,
    tiles, shifts, extents, w1, b1, w2, b2, hw, hb,
    joined, restored,
    tile, sides, landed, metas, metas_x, across, landed_x, image, stack1, first,
    w1_in, w2_in, hw_in, band1, band2, head, bias1, bias2, flat1, second,
    in_sem, send_y, recv_y, send_x, recv_x, send_m, recv_m, send_h, recv_h,
):
    p, q = lax.axis_index("gx"), lax.axis_index("gy")
    up, down = lax.rem(p + nx - 1, nx), lax.rem(p + 1, nx)
    left, right = lax.rem(q + ny - 1, ny), lax.rem(q + 1, ny)

    load = pltpu.make_async_copy(tiles.at[0, 0], tile.at[:, PAD:PAD + 40, PAD:PAD + 40], in_sem.at[0])
    load.start()
    loads = [
        pltpu.make_async_copy(w1, w1_in, in_sem.at[1]),
        pltpu.make_async_copy(w2, w2_in, in_sem.at[2]),
        pltpu.make_async_copy(hw, hw_in, in_sem.at[3]),
    ]
    for one in loads:
        one.start()
    barrier = pltpu.get_barrier_semaphore()
    is_up, is_down, is_left, is_right = p > 0, p < nx - 1, q > 0, q < ny - 1
    near = ((is_left, (p, left)), (is_right, (p, right)), (is_up, (up, q)), (is_down, (down, q)))
    for there_is, there in near:
        @pl.when(there_is)
        def _():
            pl.semaphore_signal(barrier, inc=1, device_id=there, device_id_type=MESH)

    @pl.when(q == 0)
    def _():
        landed[1] = jnp.zeros((2, 48, 16, 128), I16)
        metas_x[0, 1] = jnp.full((8, 128), -100.0, F32)
        image[:, :, 6:8] = jnp.zeros((2, 20, 2, 128), F32)

    @pl.when(q == ny - 1)
    def _():
        landed[0] = jnp.zeros((2, 48, 16, 128), I16)
        metas_x[0, 2] = jnp.full((8, 128), -100.0, F32)
        image[:, :, 24:26] = jnp.zeros((2, 20, 2, 128), F32)

    @pl.when(p == 0)
    def _():
        landed_x[1] = jnp.zeros((2, 16, 16, 128), I16)
        metas_x[1] = jnp.full((3, 8, 128), -100.0, F32)
        image[:, 0:2] = jnp.zeros((2, 2, 32, 128), F32)

    @pl.when(p == nx - 1)
    def _():
        landed_x[0] = jnp.zeros((2, 16, 16, 128), I16)
        metas_x[2] = jnp.full((3, 8, 128), -100.0, F32)
        image[:, 18:20] = jnp.zeros((2, 2, 32, 128), F32)

    tile[:, 0:PAD] = jnp.zeros((2, PAD, 56, 128), F32)
    tile[:, 48:56] = jnp.zeros((2, PAD, 56, 128), F32)
    tile[:, PAD:48, 0:PAD] = jnp.zeros((2, 40, PAD, 128), F32)
    tile[:, PAD:48, 48:56] = jnp.zeros((2, 40, PAD, 128), F32)

    s0, s1 = shifts[0, 0, 0], shifts[0, 0, 1]
    values = [shifts[0, 0, 0], shifts[0, 0, 1]] + [extents[0, 0, k] for k in range(4)]
    values = [v.astype(F32) for v in values]
    s0f, s1f, m0, m1, m2, m3 = values
    for k in range(6):
        metas[0, k:k + 1] = jnp.full((1, 128), values[k], F32)

    near_count = sum(there_is.astype(jnp.int32) for there_is, _ in near)
    pl.semaphore_wait(barrier, near_count)
    meta_copies = [
        pltpu.make_async_remote_copy(metas.at[0], metas_x.at[0, 2], send_m.at[0], recv_m.at[0],
                                     device_id=(p, left), device_id_type=MESH),
        pltpu.make_async_remote_copy(metas.at[0], metas_x.at[0, 1], send_m.at[1], recv_m.at[1],
                                     device_id=(p, right), device_id_type=MESH),
    ]
    when(is_left, meta_copies[0].start)
    when(is_right, meta_copies[1].start)
    load.wait()

    def own(r0, c0, width_vec):
        rows = ramp(iota((8, 1, 128), 0) + (r0 - 16.0) - s0f, m0, m1)
        weight = rows * width_vec
        return tile[:, pl.ds(r0 + 4 - s0 , 8), pl.ds(c0 + 4 - s1, 16), :] * weight[None]

    def columns(c0):
        return ramp(iota((1, 16, 128), 1) + (c0 - 16.0) - s1f, m2, m3)

    col_left, col_mid, col_right = columns(0), columns(16), columns(32)
    copies_y = []
    for k, r0 in enumerate(CHUNKS):
        for side, (c0, vec, there) in enumerate(((0, col_left, left), (32, col_right, right))):
            sides[side, :, r0:r0 + 8] = code(own(r0, c0, vec), STEP_Y)
            one = pltpu.make_async_remote_copy(
                sides.at[side, :, r0:r0 + 8], landed.at[side, :, r0:r0 + 8],
                send_y.at[side, k], recv_y.at[side, k], device_id=(p, there), device_id_type=MESH)
            when(is_right if side else is_left, one.start)
            copies_y.append(one)

    when(is_right, meta_copies[0].wait_recv)
    when(is_left, meta_copies[1].wait_recv)
    metas_x[0, 0] = metas[0]
    copies_m = [
        pltpu.make_async_remote_copy(metas_x.at[0], metas_x.at[2], send_m.at[2], recv_m.at[2],
                                     device_id=(up, q), device_id_type=MESH),
        pltpu.make_async_remote_copy(metas_x.at[0], metas_x.at[1], send_m.at[3], recv_m.at[3],
                                     device_id=(down, q), device_id_type=MESH),
    ]
    when(is_up, copies_m[0].start)
    when(is_down, copies_m[1].start)

    copies_x = []
    for k in range(4):
        r0 = CHUNKS[k]
        when(is_right, copies_y[2 * k].wait_recv)
        when(is_left, copies_y[2 * k + 1].wait_recv)
        side = 1 if r0 >= 32 else 0
        at = r0 - 32 if r0 >= 32 else r0
        total = own(r0, 16, col_mid)
        total = total + decode(landed[0, :, r0:r0 + 8], STEP_Y) + decode(landed[1, :, r0:r0 + 8], STEP_Y)
        across[side, :, at:at + 8] = code(total, STEP_X)
        one = pltpu.make_async_remote_copy(
            across.at[side, :, at:at + 8], landed_x.at[side, :, at:at + 8],
            send_x.at[k], recv_x.at[k], device_id=(down if side else up, q), device_id_type=MESH)
        when(is_down if side else is_up, one.start)
        copies_x.append(one)

    for one in loads:
        one.wait()
    bias1[...] = jnp.zeros((32, 128), F32)
    for k in range(32):
        bias1[k:k + 1] = jnp.full((1, 128), b1[k], F32)
        bias2[k:k + 1] = jnp.full((1, 128), b2[k], F32)
    flat1[...] = jnp.zeros((64, 32), F32)
    for dr in range(3):
        for dc in range(3):
            for dz in range(3):
                at = ((dz * 3 + dr) * 3 + dc) * 2
                flat1[at:at + 2] = w1_in[dr, dc, dz].astype(F32)
    tap = lax.broadcasted_iota(jnp.int32, (64, 256), 0)
    lane = lax.broadcasted_iota(jnp.int32, (64, 256), 1)
    target = (tap // 18) * 80 + ((tap // 6) % 3) * 16 + (tap % 2) * 8 + (tap // 2) % 3
    spread = jnp.where((lane == target) & (tap < 54), 1.0, 0.0).astype(BF16)
    strip = lax.dot_general(flat1[...].astype(BF16), spread, (((0,), (0,)), ((), ())),
                            preferred_element_type=F32)
    for orow in range(3):
        for ocol in range(6):
            at = (orow * 6 + ocol) * 32
            band1[at:at + 32] = pltpu.roll(strip, orow * 16 + ocol, 1).astype(BF16)
    zero = jnp.zeros((32, 128), BF16)
    for dz in range(3):
        strips = []
        for dr in range(3):
            taps = jnp.concatenate(
                [w2_in[dr, dc, dz].astype(F32) for dc in range(3)] + [jnp.zeros((32, 32), F32)], axis=0)
            taps = jnp.concatenate([taps, jnp.zeros((128, 96), F32)], axis=1)
            flipped = taps.T[0:32]
            strips.append((flipped.astype(BF16), pltpu.roll(flipped, 32, 1).astype(BF16)))
        for orow in range(2):
            for ocol in range(2):
                at = (orow * 2 + ocol) * 32
                for irow in range(4):
                    dr = irow - orow
                    band2[at:at + 32, dz * 512 + irow * 128:dz * 512 + irow * 128 + 128] = (
                        strips[dr][ocol] if 0 <= dr < 3 else zero)
    hrow = lax.broadcasted_iota(jnp.int32, (32, 512), 0)
    hlane = lax.broadcasted_iota(jnp.int32, (32, 512), 1)
    feat = lax.broadcasted_iota(jnp.int32, (32, 512), 0)
    pick = jnp.where(feat == hlane % 32, 1.0, 0.0).astype(BF16)
    per_lane = jnp.dot(hw_in[...], pick, preferred_element_type=F32)
    cell_row = (hlane // 64) % 2
    cell_col = (hlane // 128) * 2 + (hlane // 32) % 2
    match = ((hrow // 8) % 2 == cell_row) & (hrow % 8 == cell_col)
    by_channel = jnp.where(hrow < 16, per_lane[0:1], per_lane[1:2])
    head[...] = jnp.where(match, by_channel, 0.0).astype(BF16)

    when(is_down, copies_m[0].wait_recv)
    when(is_up, copies_m[1].wait_recv)
    for k in (4, 5):
        when(is_right, copies_y[2 * k].wait_recv)
        when(is_left, copies_y[2 * k + 1].wait_recv)
    for k, one in enumerate(copies_x):
        when(is_down if CHUNKS[k] < 32 else is_up, one.wait_recv)
    for r0 in (0, 8):
        total = own(16 + r0, 16, col_mid)
        total = total + decode(landed[0, :, 16 + r0:24 + r0], STEP_Y) + decode(landed[1, :, 16 + r0:24 + r0], STEP_Y)
        total = total + decode(landed_x[0, :, r0:r0 + 8], STEP_X) + decode(landed_x[1, :, r0:r0 + 8], STEP_X)
        weights = jnp.zeros((8, 16, 128), F32)
        for i, dp in ((0, 0), (1, -1), (2, 1)):
            for j, dq in ((0, 0), (1, -1), (2, 1)):
                meta = metas_x[i, j]
                at = [meta[k:k + 1][None] for k in range(6)]
                rows = ramp(iota((8, 1, 128), 0) + (r0 - 16.0 * dp) - at[0], at[2], at[3])
                cols = ramp(iota((1, 16, 128), 1) - 16.0 * dq - at[1], at[4], at[5])
                weights = weights + rows * cols
        cells = total / weights[None]
        joined[:, r0:r0 + 8] = cells
        image[:, 2 + r0:10 + r0, 8:24] = cells

    halo = [
        (is_up, is_down, (up, q), (slice(2, 4), slice(8, 24)), (slice(18, 20), slice(8, 24))),
        (is_down, is_up, (down, q), (slice(16, 18), slice(8, 24)), (slice(0, 2), slice(8, 24))),
        (is_left, is_right, (p, left), (slice(2, 18), slice(8, 10)), (slice(2, 18), slice(24, 26))),
        (is_right, is_left, (p, right), (slice(2, 18), slice(22, 24)), (slice(2, 18), slice(6, 8))),
        (is_up & is_left, is_down & is_right, (up, left), (slice(2, 4), slice(8, 10)), (slice(18, 20), slice(24, 26))),
        (is_up & is_right, is_down & is_left, (up, right), (slice(2, 4), slice(22, 24)), (slice(18, 20), slice(6, 8))),
        (is_down & is_left, is_up & is_right, (down, left), (slice(16, 18), slice(8, 10)), (slice(0, 2), slice(24, 26))),
        (is_down & is_right, is_up & is_left, (down, right), (slice(16, 18), slice(22, 24)), (slice(0, 2), slice(6, 8))),
    ]
    copies_h = []
    for k, (out, _, there, (rs, cs), (rd, cd)) in enumerate(halo):
        one = pltpu.make_async_remote_copy(
            image.at[:, rs, cs], image.at[:, rd, cd], send_h.at[k], recv_h.at[k],
            device_id=there, device_id_type=MESH)
        when(out, one.start)
        copies_h.append(one)
    for one, way in zip(copies_h, halo):
        when(way[1], one.wait_recv)

    for cb in range(3):
        at = 6 + 6 * cb
        cells = jnp.concatenate([image[0, :, at:at + 8], image[1, :, at:at + 8]], axis=1)
        stack1[cb, 1] = cells.astype(BF16)
        stack1[cb, 0] = shift_planes(cells, 1).astype(BF16)
        stack1[cb, 2] = shift_planes(cells, -1).astype(BF16)

    def conv1(rb, carry):
        bias = jnp.concatenate([bias1[...]] * 2, axis=1)
        for cb in range(3):
            halves = []
            for a in range(2):
                r0 = rb * 6 + a * 3
                parts = [stack1[cb, dz, pl.ds(r0, 5)].reshape(80, 128) for dz in range(3)]
                halves.append(jnp.concatenate(parts + [jnp.zeros((16, 128), BF16)], axis=0))
            out = jnp.dot(band1[...], jnp.concatenate(halves, axis=1), preferred_element_type=F32)
            out = jnp.maximum(out.reshape(18, 32, 256) + bias[None], 0.0)
            for dz in range(3):
                one = out if dz == 1 else shift_planes(out, 1 - dz)
                one = one.astype(BF16).reshape(3, 6, 32, 256)
                for a in range(2):
                    first[dz, pl.ds(rb * 6 + a * 3, 3), cb * 6:cb * 6 + 6] = one[:, :, :, a * 128:a * 128 + 128]
        return carry

    lax.fori_loop(0, 3, conv1, 0)

    @pl.when(p == 0)
    def _():
        first[:, 0:1] = jnp.zeros((3, 1, 18, 32, 128), BF16)

    @pl.when(p == nx - 1)
    def _():
        first[:, 17:18] = jnp.zeros((3, 1, 18, 32, 128), BF16)

    @pl.when(q == 0)
    def _():
        first[:, :, 0:1] = jnp.zeros((3, 18, 1, 32, 128), BF16)

    @pl.when(q == ny - 1)
    def _():
        first[:, :, 17:18] = jnp.zeros((3, 18, 1, 32, 128), BF16)

    bias = jnp.concatenate([jnp.concatenate([bias2[...]] * 4, axis=0)] * 4, axis=1)

    def project(step):
        quad, half = step // 2, step % 2
        out = jnp.dot(head[...], second[:, step * 256:step * 256 + 256], preferred_element_type=F32)
        for ch in range(2):
            for a in range(2):
                for r in range(2):
                    at = ch * 16 + r * 8
                    restored[ch, quad * 4 + 2 * a + r, half * 8:half * 8 + 8, :] = (
                        out[at:at + 8, a * 128:a * 128 + 128] + hb[ch])

    for step in range(8):
        quad, half = step // 2, step % 2
        for b0 in (0, 2):
            cols = []
            for b in (b0, b0 + 1):
                c0 = half * 8 + 2 * b
                for a in range(2):
                    r0 = quad * 4 + 2 * a
                    cols.append(jnp.concatenate(
                        [first[dz, r0:r0 + 4, c0:c0 + 4].reshape(512, 128) for dz in range(3)], axis=0))
            out = jnp.dot(band2[...], jnp.concatenate(cols, axis=1), preferred_element_type=F32)
            out = jnp.maximum(out + bias, 0.0).astype(BF16)
            for j in range(2):
                second[(b0 + j) * 128:(b0 + j) * 128 + 128, step * 256:step * 256 + 256] = (
                    out[:, j * 256:j * 256 + 256])
        if step > 0:
            project(step - 1)
    project(7)

    when(is_left, meta_copies[0].wait_send)
    when(is_right, meta_copies[1].wait_send)
    for k, one in enumerate(copies_y):
        when(is_right if k % 2 else is_left, one.wait_send)
    when(is_up, copies_m[0].wait_send)
    when(is_down, copies_m[1].wait_send)
    for k, one in enumerate(copies_x):
        when(is_down if CHUNKS[k] >= 32 else is_up, one.wait_send)
    for one, way in zip(copies_h, halo):
        when(way[0], one.wait_send)


def shards(tiles, shifts, extents, w1, b1, w2, b2, hw, hb):
    nx, ny = lax.axis_size("gx"), lax.axis_size("gy")
    vmem = pl.BlockSpec(memory_space=pltpu.VMEM)
    smem = pl.BlockSpec(memory_space=pltpu.SMEM)
    hbm = pl.BlockSpec(memory_space=pl.ANY)

    def body(*refs):
        kernel(nx, ny, *refs)

    dma = pltpu.SemaphoreType.DMA
    return pl.pallas_call(
        body,
        out_shape=[pltpu.VMEM((2, 16, 16, 128), F32)] * 2,
        in_specs=[hbm, smem, smem, hbm, smem, hbm, smem, hbm, smem],
        out_specs=[vmem, vmem],
        scratch_shapes=[
            pltpu.VMEM((2, 56, 56, 128), F32),
            pltpu.VMEM((2, 2, 48, 16, 128), I16),
            pltpu.VMEM((2, 2, 48, 16, 128), I16),
            pltpu.VMEM((1, 8, 128), F32),
            pltpu.VMEM((3, 3, 8, 128), F32),
            pltpu.VMEM((2, 2, 16, 16, 128), I16),
            pltpu.VMEM((2, 2, 16, 16, 128), I16),
            pltpu.VMEM((2, 20, 32, 128), F32),
            pltpu.VMEM((3, 3, 20, 16, 128), BF16),
            pltpu.VMEM((3, 18, 18, 32, 128), BF16),
            pltpu.VMEM((3, 3, 3, 2, 32), BF16),
            pltpu.VMEM((3, 3, 3, 32, 32), BF16),
            pltpu.VMEM((2, 32), BF16),
            pltpu.VMEM((576, 256), BF16),
            pltpu.VMEM((128, 1536), BF16),
            pltpu.VMEM((32, 512), BF16),
            pltpu.VMEM((32, 128), F32),
            pltpu.VMEM((32, 128), F32),
            pltpu.VMEM((64, 32), F32),
            pltpu.VMEM((512, 2048), BF16),
            dma((4,)), dma((2, 6)), dma((2, 6)), dma((4,)), dma((4,)), dma((4,)), dma((4,)), dma((8,)), dma((8,)),
        ],
        compiler_params=pltpu.CompilerParams(
            collective_id=0, has_side_effects=True, vmem_limit_bytes=60 * 1024 * 1024),
    )(tiles, shifts, extents, w1, b1, w2, b2, hw.T, hb)


def solution(mesh):
    return jax.shard_map(
        shards,
        mesh=mesh,
        in_specs=(P("gx", "gy"), P("gx", "gy"), P("gx", "gy"), P(), P(), P(), P(), P(), P()),
        out_specs=(P(None, "gx", "gy", None), P(None, "gx", "gy", None)),
        check_vma=False,
    )
```

```python
import jax
import jax.numpy as jnp
from jax import lax
from jax.experimental import pallas as pl
from jax.experimental.pallas import tpu as pltpu
from jax.sharding import PartitionSpec as P

MESH = pl.DeviceIdType.MESH
F32 = jnp.float32
BF16 = jnp.bfloat16
I16 = jnp.int16
STEP_Y = 4.0 / 32767
STEP_X = 12.0 / 32767
PAD = 8
CHUNKS = ((32, 8), (0, 8), (40, 8), (8, 8), (30, 2), (16, 2), (18, 6), (24, 6))
COLUMNS = (0, 1, 4, 5, 2, 3)


def ramp(places, before, after):
    rise = places + 1.0 + before
    fall = 16.0 + after - places
    return jnp.clip(jnp.minimum(rise, fall), 0.0, 8.0) * 0.125


def code(values, step):
    return jnp.round(values * (1.0 / step)).astype(jnp.int32).astype(I16)


def decode(values, step):
    return values.astype(jnp.int32).astype(F32) * step


def when(condition, action):
    pl.when(condition)(action)


def shift_planes(x, by):
    lane = lax.broadcasted_iota(jnp.int32, x.shape[:-1] + (128,), x.ndim - 1)
    parts = []
    for g in range(x.shape[-1] // 128):
        one = pltpu.roll(x[..., g * 128:g * 128 + 128], by % 128, x.ndim - 1)
        parts.append(jnp.where(lane == (0 if by > 0 else 127), 0.0, one))
    return jnp.concatenate(parts, axis=-1)


def iota(shape, dim):
    return lax.broadcasted_iota(jnp.int32, shape, dim).astype(F32)


def kernel(
    nx, ny,
    tiles, shifts, extents, w1, b1, w2, b2, hw, hb,
    joined, restored,
    tile, sides, landed, metas, metas_x, across, landed_x, landed_far, image, stack1, first,
    w1_in, w2_in, hw_in, band1, band2, head, bias1, bias2, flat1, second, inverse,
    in_sem, send_y, recv_y, send_x, recv_x, send_m, recv_m, send_h, recv_h,
):
    p, q = lax.axis_index("gx"), lax.axis_index("gy")
    up, down = lax.rem(p + nx - 1, nx), lax.rem(p + 1, nx)
    up2, down2 = lax.rem(p + nx - 2, nx), lax.rem(p + 2, nx)
    left, right = lax.rem(q + ny - 1, ny), lax.rem(q + 1, ny)

    load = pltpu.make_async_copy(tiles.at[0, 0], tile.at[:, PAD:PAD + 40, PAD:PAD + 40], in_sem.at[0])
    load.start()
    loads = [
        pltpu.make_async_copy(w1, w1_in, in_sem.at[1]),
        pltpu.make_async_copy(w2, w2_in, in_sem.at[2]),
        pltpu.make_async_copy(hw, hw_in, in_sem.at[3]),
    ]
    for one in loads:
        one.start()
    barrier = pltpu.get_barrier_semaphore()
    is_up, is_down, is_left, is_right = p > 0, p < nx - 1, q > 0, q < ny - 1
    is_up2, is_down2 = p > 1, p < nx - 2
    near = ((is_left, (p, left)), (is_right, (p, right)), (is_up, (up, q)), (is_down, (down, q)))
    for there_is, there in near:
        @pl.when(there_is)
        def _():
            pl.semaphore_signal(barrier, inc=1, device_id=there, device_id_type=MESH)

    @pl.when(q == 0)
    def _():
        landed[1] = jnp.zeros((2, 48, 16, 128), I16)
        metas_x[2, 1] = jnp.full((8, 128), -100.0, F32)
        image[:, :, 6:8] = jnp.zeros((2, 20, 2, 128), F32)

    @pl.when(q == ny - 1)
    def _():
        landed[0] = jnp.zeros((2, 48, 16, 128), I16)
        metas_x[2, 2] = jnp.full((8, 128), -100.0, F32)
        image[:, :, 24:26] = jnp.zeros((2, 20, 2, 128), F32)

    @pl.when(p == 0)
    def _():
        landed_x[1] = jnp.zeros((2, 18, 16, 128), I16)
        metas_x[1] = jnp.full((3, 8, 128), -100.0, F32)

    @pl.when(p == nx - 1)
    def _():
        landed_x[0] = jnp.zeros((2, 18, 16, 128), I16)
        metas_x[3] = jnp.full((3, 8, 128), -100.0, F32)

    @pl.when(p <= 1)
    def _():
        landed_far[1] = jnp.zeros((2, 2, 16, 128), I16)
        metas_x[0] = jnp.full((3, 8, 128), -100.0, F32)

    @pl.when(p >= nx - 2)
    def _():
        landed_far[0] = jnp.zeros((2, 2, 16, 128), I16)
        metas_x[4] = jnp.full((3, 8, 128), -100.0, F32)

    tile[:, 0:PAD] = jnp.zeros((2, PAD, 56, 128), F32)
    tile[:, 48:56] = jnp.zeros((2, PAD, 56, 128), F32)
    tile[:, PAD:48, 0:PAD] = jnp.zeros((2, 40, PAD, 128), F32)
    tile[:, PAD:48, 48:56] = jnp.zeros((2, 40, PAD, 128), F32)

    s0, s1 = shifts[0, 0, 0], shifts[0, 0, 1]
    values = [shifts[0, 0, 0], shifts[0, 0, 1]] + [extents[0, 0, k] for k in range(4)]
    values = [v.astype(F32) for v in values]
    s0f, s1f, m0, m1, m2, m3 = values
    for k in range(6):
        metas[0, k:k + 1] = jnp.full((1, 128), values[k], F32)

    near_count = sum(there_is.astype(jnp.int32) for there_is, _ in near)
    pl.semaphore_wait(barrier, near_count)
    meta_copies = [
        pltpu.make_async_remote_copy(metas.at[0], metas_x.at[2, 2], send_m.at[0], recv_m.at[0],
                                     device_id=(p, left), device_id_type=MESH),
        pltpu.make_async_remote_copy(metas.at[0], metas_x.at[2, 1], send_m.at[1], recv_m.at[1],
                                     device_id=(p, right), device_id_type=MESH),
    ]
    when(is_left, meta_copies[0].start)
    when(is_right, meta_copies[1].start)
    load.wait()

    def own(r0, count, c0, width_vec):
        rows = ramp(iota((count, 1, 128), 0) + (r0 - 16.0) - s0f, m0, m1)
        weight = rows * width_vec
        return tile[:, pl.ds(r0 + 4 - s0 , count), pl.ds(c0 + 4 - s1, 16), :] * weight[None]

    def row_sum(r0, count):
        total = own(r0, count, 16, col_mid)
        total = total + decode(landed[0, :, r0:r0 + count], STEP_Y)
        return total + decode(landed[1, :, r0:r0 + count], STEP_Y)

    def columns(c0):
        return ramp(iota((1, 16, 128), 1) + (c0 - 16.0) - s1f, m2, m3)

    col_left, col_mid, col_right = columns(0), columns(16), columns(32)
    copies_y = []
    for k, (r0, count) in enumerate(CHUNKS):
        for side, (c0, vec, there) in enumerate(((0, col_left, left), (32, col_right, right))):
            sides[side, :, r0:r0 + count] = code(own(r0, count, c0, vec), STEP_Y)
            one = pltpu.make_async_remote_copy(
                sides.at[side, :, r0:r0 + count], landed.at[side, :, r0:r0 + count],
                send_y.at[side, k], recv_y.at[side, k], device_id=(p, there), device_id_type=MESH)
            when(is_right if side else is_left, one.start)
            copies_y.append(one)

    when(is_right, meta_copies[0].wait_recv)
    when(is_left, meta_copies[1].wait_recv)
    metas_x[2, 0] = metas[0]
    copies_m = [
        pltpu.make_async_remote_copy(metas_x.at[2], metas_x.at[2 + by], send_m.at[k], recv_m.at[k],
                                     device_id=(there, q), device_id_type=MESH)
        for k, by, there in ((2, 1, up), (3, -1, down), (4, 2, up2), (5, -2, down2))
    ]
    when(is_up, copies_m[0].start)
    when(is_down, copies_m[1].start)

    copies_x, ways_x = [], []

    def across_copy(src, dst, out, back, there):
        k = len(copies_x)
        one = pltpu.make_async_remote_copy(src, dst, send_x.at[k], recv_x.at[k],
                                           device_id=(there, q), device_id_type=MESH)
        when(out, one.start)
        copies_x.append(one)
        ways_x.append((out, back))

    for k in range(6):
        r0, count = CHUNKS[k]
        when(is_right, copies_y[2 * k].wait_recv)
        when(is_left, copies_y[2 * k + 1].wait_recv)
        side = 1 if r0 >= 30 else 0
        at = r0 - 30 * side
        across[side, :, at:at + count] = code(row_sum(r0, count), STEP_X)
        across_copy(across.at[side, :, at:at + count], landed_x.at[side, :, at:at + count],
                    is_down if side else is_up, is_up if side else is_down, down if side else up)
        if k == 3:
            when(is_down, copies_m[0].wait_recv)
            when(is_up, copies_m[1].wait_recv)
            when(is_up2, copies_m[2].start)
            when(is_down2, copies_m[3].start)
            across_copy(across.at[1, :, 16:18], landed_far.at[1], is_down2, is_up2, down2)
            across_copy(across.at[0, :, 0:2], landed_far.at[0], is_up2, is_down2, up2)

    for one in loads:
        one.wait()
    bias1[...] = jnp.zeros((32, 128), F32)
    for k in range(32):
        bias1[k:k + 1] = jnp.full((1, 128), b1[k], F32)
        bias2[k:k + 1] = jnp.full((1, 128), b2[k], F32)
    flat1[...] = jnp.zeros((64, 32), F32)
    for dr in range(3):
        for dc in range(3):
            for dz in range(3):
                at = ((dz * 3 + dr) * 3 + dc) * 2
                flat1[at:at + 2] = w1_in[dr, dc, dz].astype(F32)
    tap = lax.broadcasted_iota(jnp.int32, (64, 256), 0)
    lane = lax.broadcasted_iota(jnp.int32, (64, 256), 1)
    target = (tap // 18) * 80 + ((tap // 6) % 3) * 16 + (tap % 2) * 8 + (tap // 2) % 3
    spread = jnp.where((lane == target) & (tap < 54), 1.0, 0.0).astype(BF16)
    strip = lax.dot_general(flat1[...].astype(BF16), spread, (((0,), (0,)), ((), ())),
                            preferred_element_type=F32)
    for i, ocol in enumerate(COLUMNS):
        for orow in range(3):
            at = (i * 3 + orow) * 32
            band1[at:at + 32] = pltpu.roll(strip, orow * 16 + ocol, 1).astype(BF16)
    zero = jnp.zeros((32, 128), BF16)
    for dz in range(3):
        strips = []
        for dr in range(3):
            taps = jnp.concatenate(
                [w2_in[dr, dc, dz].astype(F32) for dc in range(3)] + [jnp.zeros((32, 32), F32)], axis=0)
            taps = jnp.concatenate([taps, jnp.zeros((128, 96), F32)], axis=1)
            flipped = taps.T[0:32]
            strips.append((flipped.astype(BF16), pltpu.roll(flipped, 32, 1).astype(BF16)))
        for orow in range(2):
            for ocol in range(2):
                at = (orow * 2 + ocol) * 32
                for irow in range(4):
                    dr = irow - orow
                    band2[at:at + 32, dz * 512 + irow * 128:dz * 512 + irow * 128 + 128] = (
                        strips[dr][ocol] if 0 <= dr < 3 else zero)
    hrow = lax.broadcasted_iota(jnp.int32, (32, 512), 0)
    hlane = lax.broadcasted_iota(jnp.int32, (32, 512), 1)
    feat = lax.broadcasted_iota(jnp.int32, (32, 512), 0)
    pick = jnp.where(feat == hlane % 32, 1.0, 0.0).astype(BF16)
    per_lane = jnp.dot(hw_in[...], pick, preferred_element_type=F32)
    cell_row = (hlane // 64) % 2
    cell_col = (hlane // 128) * 2 + (hlane // 32) % 2
    match = ((hrow // 8) % 2 == cell_row) & (hrow % 8 == cell_col)
    by_channel = jnp.where(hrow < 16, per_lane[0:1], per_lane[1:2])
    head[...] = jnp.where(match, by_channel, 0.0).astype(BF16)

    when(is_down2, copies_m[2].wait_recv)
    when(is_up2, copies_m[3].wait_recv)
    parts = ((0, 2, (-2, -1, 0)), (2, 8, (-1, 0, 1)), (10, 8, (-1, 0, 1)), (18, 2, (0, 1, 2)))
    for r0, count, reach in parts:
        weights = jnp.zeros((count, 16, 128), F32)
        for dp in reach:
            for j, dq in ((0, 0), (1, -1), (2, 1)):
                meta = metas_x[2 + dp, j]
                at = [meta[k:k + 1][None] for k in range(6)]
                rows = ramp(iota((count, 1, 128), 0) + (r0 - 2 - 16.0 * dp) - at[0], at[2], at[3])
                cols = ramp(iota((1, 16, 128), 1) - 16.0 * dq - at[1], at[4], at[5])
                weights = weights + rows * cols
        inverse[r0:r0 + count] = 1.0 / weights

    for k in (6, 7):
        when(is_right, copies_y[2 * k].wait_recv)
        when(is_left, copies_y[2 * k + 1].wait_recv)
    for one, way in zip(copies_x, ways_x):
        when(way[1], one.wait_recv)
    for r0, count, reach in parts:
        total = row_sum(14 + r0, count)
        if r0 < 18:
            total = total + decode(landed_x[1, :, r0:r0 + count], STEP_X)
        else:
            total = total + decode(landed_far[0], STEP_X)
        if r0 >= 2:
            total = total + decode(landed_x[0, :, r0 - 2:r0 - 2 + count], STEP_X)
        else:
            total = total + decode(landed_far[1], STEP_X)
        cells = total * inverse[r0:r0 + count][None]
        image[:, r0:r0 + count, 8:24] = cells
        if count == 8:
            joined[:, r0 - 2:r0 + 6] = cells

    @pl.when(p == 0)
    def _():
        image[:, 0:2, 8:24] = jnp.zeros((2, 2, 16, 128), F32)

    @pl.when(p == nx - 1)
    def _():
        image[:, 18:20, 8:24] = jnp.zeros((2, 2, 16, 128), F32)

    copies_h = [
        pltpu.make_async_remote_copy(
            image.at[:, :, src:src + 2], image.at[:, :, dst:dst + 2], send_h.at[k], recv_h.at[k],
            device_id=(p, there), device_id_type=MESH)
        for k, src, dst, there in ((0, 8, 24, left), (1, 22, 6, right))
    ]
    when(is_left, copies_h[0].start)
    when(is_right, copies_h[1].start)

    def stack(block, cells):
        stack1[block, 1] = cells.astype(BF16)
        stack1[block, 0] = shift_planes(cells, 1).astype(BF16)
        stack1[block, 2] = shift_planes(cells, -1).astype(BF16)

    def conv1(block, rows, low, high, places):
        halves = []
        for r0 in rows:
            parts = [stack1[block, dz, pl.ds(r0, 5)].reshape(80, 128) for dz in range(3)]
            halves.append(jnp.concatenate(parts + [jnp.zeros((16, 128), BF16)], axis=0))
        count, lanes = (high - low) // 96, 128 * len(rows)
        bias = jnp.concatenate([bias1[...]] * len(rows), axis=1)
        out = jnp.dot(band1[low:high], jnp.concatenate(halves, axis=1), preferred_element_type=F32)
        out = jnp.maximum(out.reshape(3 * count, 32, lanes) + bias[None], 0.0)
        for dz in range(3):
            one = out if dz == 1 else shift_planes(out, 1 - dz)
            one = one.astype(BF16).reshape(count, 3, 32, lanes)
            for a, r0 in enumerate(rows):
                for i, place in enumerate(places):
                    first[dz, pl.ds(r0, 3), place] = one[i, :, :, a * 128:a * 128 + 128]

    for block, at in ((0, 8), (1, 14), (2, 16)):
        stack(block, jnp.concatenate([image[0, :, at:at + 8], image[1, :, at:at + 8]], axis=1))

    def inner(i, carry):
        rows = (i * 6, i * 6 + 3)
        conv1(0, rows, 0, 576, [2 + c for c in COLUMNS])
        conv1(1, rows, 0, 576, [8 + c for c in COLUMNS])
        conv1(2, rows, 192, 384, [14, 15])
        return carry

    lax.fori_loop(0, 3, inner, 0)

    def clear_rows(low, high):
        @pl.when(p == 0)
        def _():
            first[:, 0:1, low:high] = jnp.zeros((3, 1, high - low, 32, 128), BF16)

        @pl.when(p == nx - 1)
        def _():
            first[:, 17:18, low:high] = jnp.zeros((3, 1, high - low, 32, 128), BF16)

    clear_rows(2, 16)

    bias = jnp.concatenate([jnp.concatenate([bias2[...]] * 4, axis=0)] * 4, axis=1)

    def conv2(quad, blocks, slot, b0):
        cols = []
        for c0 in blocks:
            for a in range(2):
                r0 = quad * 4 + 2 * a
                cols.append(jnp.concatenate(
                    [first[dz, r0:r0 + 4, c0:c0 + 4].reshape(512, 128) for dz in range(3)], axis=0))
        out = jnp.dot(band2[...], jnp.concatenate(cols, axis=1), preferred_element_type=F32)
        out = jnp.maximum(out + bias, 0.0).astype(BF16)
        for j in range(2):
            second[(b0 + j) * 128:(b0 + j) * 128 + 128, slot * 256:slot * 256 + 256] = (
                out[:, j * 256:j * 256 + 256])

    def project(quad, slot, places):
        out = jnp.dot(head[...], second[:, slot * 256:slot * 256 + 256], preferred_element_type=F32)
        for ch in range(2):
            for a in range(2):
                for r in range(2):
                    cells = out[ch * 16 + r * 8:ch * 16 + r * 8 + 8, a * 128:a * 128 + 128] + hb[ch]
                    for src, dst, count in places:
                        restored[ch, quad * 4 + 2 * a + r, dst:dst + count, :] = cells[src:src + count]

    for quad in range(4):
        conv2(quad, (2, 4), quad, 0)
        conv2(quad, (6, 8), quad, 2)
        conv2(quad, (10, 12), 4 + quad, 0)
        if quad > 0:
            project(quad - 1, quad - 1, ((0, 2, 8),))

    when(is_right, copies_h[0].wait_recv)
    when(is_left, copies_h[1].wait_recv)
    stack(3, jnp.concatenate(
        [image[0, :, 6:10], image[0, :, 22:26], image[1, :, 6:10], image[1, :, 22:26]], axis=1))
    conv1(3, (0, 3, 6, 9, 12, 15), 0, 384, [0, 1, 16, 17])
    clear_rows(0, 18)

    @pl.when(q == 0)
    def _():
        first[:, :, 0:1] = jnp.zeros((3, 18, 1, 32, 128), BF16)

    @pl.when(q == ny - 1)
    def _():
        first[:, :, 17:18] = jnp.zeros((3, 18, 1, 32, 128), BF16)

    project(3, 3, ((0, 2, 8),))
    for quad in range(4):
        conv2(quad, (0, 14), 4 + quad, 2)
        if quad > 0:
            project(quad - 1, 3 + quad, ((0, 10, 4), (4, 0, 2), (6, 14, 2)))
    project(3, 7, ((0, 10, 4), (4, 0, 2), (6, 14, 2)))

    when(is_left, meta_copies[0].wait_send)
    when(is_right, meta_copies[1].wait_send)
    for k, one in enumerate(copies_y):
        when(is_right if k % 2 else is_left, one.wait_send)
    for one, way in zip(copies_m, (is_up, is_down, is_up2, is_down2)):
        when(way, one.wait_send)
    for one, way in zip(copies_x, ways_x):
        when(way[0], one.wait_send)
    when(is_left, copies_h[0].wait_send)
    when(is_right, copies_h[1].wait_send)


def shards(tiles, shifts, extents, w1, b1, w2, b2, hw, hb):
    nx, ny = lax.axis_size("gx"), lax.axis_size("gy")
    vmem = pl.BlockSpec(memory_space=pltpu.VMEM)
    smem = pl.BlockSpec(memory_space=pltpu.SMEM)
    hbm = pl.BlockSpec(memory_space=pl.ANY)

    def body(*refs):
        kernel(nx, ny, *refs)

    dma = pltpu.SemaphoreType.DMA
    return pl.pallas_call(
        body,
        out_shape=[pltpu.VMEM((2, 16, 16, 128), F32)] * 2,
        in_specs=[hbm, smem, smem, hbm, smem, hbm, smem, hbm, smem],
        out_specs=[vmem, vmem],
        scratch_shapes=[
            pltpu.VMEM((2, 56, 56, 128), F32),
            pltpu.VMEM((2, 2, 48, 16, 128), I16),
            pltpu.VMEM((2, 2, 48, 16, 128), I16),
            pltpu.VMEM((1, 8, 128), F32),
            pltpu.VMEM((5, 3, 8, 128), F32),
            pltpu.VMEM((2, 2, 18, 16, 128), I16),
            pltpu.VMEM((2, 2, 18, 16, 128), I16),
            pltpu.VMEM((2, 2, 2, 16, 128), I16),
            pltpu.VMEM((2, 20, 32, 128), F32),
            pltpu.VMEM((4, 3, 20, 16, 128), BF16),
            pltpu.VMEM((3, 18, 18, 32, 128), BF16),
            pltpu.VMEM((3, 3, 3, 2, 32), BF16),
            pltpu.VMEM((3, 3, 3, 32, 32), BF16),
            pltpu.VMEM((2, 32), BF16),
            pltpu.VMEM((576, 256), BF16),
            pltpu.VMEM((128, 1536), BF16),
            pltpu.VMEM((32, 512), BF16),
            pltpu.VMEM((32, 128), F32),
            pltpu.VMEM((32, 128), F32),
            pltpu.VMEM((64, 32), F32),
            pltpu.VMEM((512, 2048), BF16),
            pltpu.VMEM((20, 16, 128), F32),
            dma((4,)), dma((2, 8)), dma((2, 8)), dma((8,)), dma((8,)), dma((6,)), dma((6,)), dma((2,)), dma((2,)),
        ],
        compiler_params=pltpu.CompilerParams(
            collective_id=0, has_side_effects=True, vmem_limit_bytes=60 * 1024 * 1024),
    )(tiles, shifts, extents, w1, b1, w2, b2, hw.T, hb)


def solution(mesh):
    return jax.shard_map(
        shards,
        mesh=mesh,
        in_specs=(P("gx", "gy"), P("gx", "gy"), P("gx", "gy"), P(), P(), P(), P(), P(), P()),
        out_specs=(P(None, "gx", "gy", None), P(None, "gx", "gy", None)),
        check_vma=False,
    )
```

```python
import jax
import jax.numpy as jnp
from jax import lax
from jax.experimental import pallas as pl
from jax.experimental.pallas import tpu as pltpu
from jax.sharding import PartitionSpec as P

MESH = pl.DeviceIdType.MESH
F32 = jnp.float32
BF16 = jnp.bfloat16
I16 = jnp.int16
STEP_Y = 4.0 / 32767
STEP_X = 12.0 / 32767
PAD = 8
CHUNKS = ((32, 8), (0, 8), (40, 8), (8, 8), (30, 2), (16, 2), (18, 6), (24, 6))
FOLDED = 6
MAIN = 4
COLUMNS = (0, 1, 4, 5, 2, 3)


def ramp(places, before, after):
    rise = places + 1.0 + before
    fall = 16.0 + after - places
    return jnp.clip(jnp.minimum(rise, fall), 0.0, 8.0) * 0.125


def code(values, step):
    return (values * (1.0 / step) + 0.5).astype(jnp.int32).astype(I16)


def decode(values, step):
    return values.astype(jnp.int32).astype(F32) * step


def when(condition, action):
    pl.when(condition)(action)


def shift_planes(x, by):
    lane = lax.broadcasted_iota(jnp.int32, x.shape[:-1] + (128,), x.ndim - 1)
    parts = []
    for g in range(x.shape[-1] // 128):
        one = pltpu.roll(x[..., g * 128:g * 128 + 128], by % 128, x.ndim - 1)
        parts.append(jnp.where(lane == (0 if by > 0 else 127), jnp.zeros_like(one), one))
    return jnp.concatenate(parts, axis=-1)


def iota(shape, dim):
    return lax.broadcasted_iota(jnp.int32, shape, dim).astype(F32)


def kernel(
    nx, ny,
    tiles, shifts_in, extents_in, w1, b1_in, w2, b2_in, hw, hb_in,
    joined, restored,
    tile, sides, landed, metas, metas_x, across, landed_x, landed_far, image, stack1, first,
    w1_in, w2_in, hw_in, band1, band2, head, bias1, bias2, flat1, second, inverse, shifts, extents, b1, b2, hb, small_sem,
    in_sem, send_y, recv_y, send_x, recv_x, send_m, recv_m, send_h, recv_h,
):
    p, q = lax.axis_index("gx"), lax.axis_index("gy")
    up, down = lax.rem(p + nx - 1, nx), lax.rem(p + 1, nx)
    up2, down2 = lax.rem(p + nx - 2, nx), lax.rem(p + 2, nx)
    left, right = lax.rem(q + ny - 1, ny), lax.rem(q + 1, ny)

    barrier = pltpu.get_barrier_semaphore()
    is_up, is_down, is_left, is_right = p > 0, p < nx - 1, q > 0, q < ny - 1
    is_up2, is_down2 = p > 1, p < nx - 2
    near = ((is_left, (p, left)), (is_right, (p, right)), (is_up, (up, q)), (is_down, (down, q)))
    for there_is, there in near:
        @pl.when(there_is)
        def _():
            pl.semaphore_signal(barrier, inc=1, device_id=there, device_id_type=MESH)

    small = [
        pltpu.make_async_copy(src, dst, small_sem.at[k])
        for k, (src, dst) in enumerate(
            ((shifts_in, shifts), (extents_in, extents), (b1_in, b1), (b2_in, b2), (hb_in, hb)))
    ]
    for one in small:
        one.start()
    load = pltpu.make_async_copy(tiles.at[0, 0], tile.at[:, PAD:PAD + 40, PAD:PAD + 40], in_sem.at[0])
    load.start()
    loads = [
        pltpu.make_async_copy(w1, w1_in, in_sem.at[1]),
        pltpu.make_async_copy(w2, w2_in, in_sem.at[2]),
        pltpu.make_async_copy(hw, hw_in, in_sem.at[3]),
    ]
    for one in loads:
        one.start()
    @pl.when(q == 0)
    def _():
        landed[1] = jnp.zeros((2, 48, 16, 128), I16)
        metas_x[2, 1] = jnp.full((8, 128), -100.0, F32)
        image[:, :, 6:8] = jnp.zeros((2, 20, 2, 128), F32)

    @pl.when(q == ny - 1)
    def _():
        landed[0] = jnp.zeros((2, 48, 16, 128), I16)
        metas_x[2, 2] = jnp.full((8, 128), -100.0, F32)
        image[:, :, 24:26] = jnp.zeros((2, 20, 2, 128), F32)

    @pl.when(p == 0)
    def _():
        landed_x[1] = jnp.zeros((2, 18, 16, 128), I16)
        metas_x[1] = jnp.full((3, 8, 128), -100.0, F32)

    @pl.when(p == nx - 1)
    def _():
        landed_x[0] = jnp.zeros((2, 18, 16, 128), I16)
        metas_x[3] = jnp.full((3, 8, 128), -100.0, F32)

    @pl.when(p <= 1)
    def _():
        landed_far[1] = jnp.zeros((2, 2, 16, 128), I16)
        metas_x[0] = jnp.full((3, 8, 128), -100.0, F32)

    @pl.when(p >= nx - 2)
    def _():
        landed_far[0] = jnp.zeros((2, 2, 16, 128), I16)
        metas_x[4] = jnp.full((3, 8, 128), -100.0, F32)

    tile[:, 0:PAD] = jnp.zeros((2, PAD, 56, 128), F32)
    tile[:, 48:56] = jnp.zeros((2, PAD, 56, 128), F32)
    tile[:, PAD:48, 0:PAD] = jnp.zeros((2, 40, PAD, 128), F32)
    tile[:, PAD:48, 48:56] = jnp.zeros((2, 40, PAD, 128), F32)

    small[0].wait()
    small[1].wait()
    s0, s1 = shifts[0, 0, 0], shifts[0, 0, 1]
    values = [shifts[0, 0, 0], shifts[0, 0, 1]] + [extents[0, 0, k] for k in range(4)]
    values = [v.astype(F32) for v in values]
    s0f, s1f, m0, m1, m2, m3 = values
    for k in range(6):
        metas[0, k:k + 1] = jnp.full((1, 128), values[k], F32)

    near_count = sum(there_is.astype(jnp.int32) for there_is, _ in near)
    pl.semaphore_wait(barrier, near_count)
    meta_copies = [
        pltpu.make_async_remote_copy(metas.at[0], metas_x.at[2, 2], send_m.at[0], recv_m.at[0],
                                     device_id=(p, left), device_id_type=MESH),
        pltpu.make_async_remote_copy(metas.at[0], metas_x.at[2, 1], send_m.at[1], recv_m.at[1],
                                     device_id=(p, right), device_id_type=MESH),
    ]
    when(is_left, meta_copies[0].start)
    when(is_right, meta_copies[1].start)
    load.wait()

    def own(r0, count, c0, width_vec):
        rows = ramp(iota((count, 1, 128), 0) + (r0 - 16.0) - s0f, m0, m1)
        weight = rows * width_vec
        return tile[:, pl.ds(r0 + 4 - s0 , count), pl.ds(c0 + 4 - s1, 16), :] * weight[None]

    def row_sum(r0, count):
        total = own(r0, count, 16, col_mid)
        total = total + decode(landed[0, :, r0:r0 + count], STEP_Y)
        return total + decode(landed[1, :, r0:r0 + count], STEP_Y)

    def columns(c0):
        return ramp(iota((1, 16, 128), 1) + (c0 - 16.0) - s1f, m2, m3)

    col_left, col_mid, col_right = columns(0), columns(16), columns(32)
    copies_y = []
    for k, (r0, count) in enumerate(CHUNKS):
        for side, (c0, vec, there) in enumerate(((0, col_left, left), (32, col_right, right))):
            sides[side, :, r0:r0 + count] = code(own(r0, count, c0, vec), STEP_Y)
            one = pltpu.make_async_remote_copy(
                sides.at[side, :, r0:r0 + count], landed.at[side, :, r0:r0 + count],
                send_y.at[side, k], recv_y.at[side, k], device_id=(p, there), device_id_type=MESH)
            when(is_right if side else is_left, one.start)
            copies_y.append(one)

    when(is_right, meta_copies[0].wait_recv)
    when(is_left, meta_copies[1].wait_recv)
    metas_x[2, 0] = metas[0]
    copies_m = [
        pltpu.make_async_remote_copy(metas_x.at[2], metas_x.at[2 + by], send_m.at[k], recv_m.at[k],
                                     device_id=(there, q), device_id_type=MESH)
        for k, by, there in ((2, 1, up), (3, -1, down), (4, 2, up2), (5, -2, down2))
    ]
    when(is_up, copies_m[0].start)
    when(is_down, copies_m[1].start)

    copies_x, ways_x = [], []

    def across_copy(src, dst, out, back, there):
        k = len(copies_x)
        one = pltpu.make_async_remote_copy(src, dst, send_x.at[k], recv_x.at[k],
                                           device_id=(there, q), device_id_type=MESH)
        when(out, one.start)
        copies_x.append(one)
        ways_x.append((out, back))

    for k in range(FOLDED):
        r0, count = CHUNKS[k]
        when(is_right, copies_y[2 * k].wait_recv)
        when(is_left, copies_y[2 * k + 1].wait_recv)
        side = 1 if r0 >= 30 else 0
        at = r0 - 30 * side
        across[side, :, at:at + count] = code(row_sum(r0, count), STEP_X)
        across_copy(across.at[side, :, at:at + count], landed_x.at[side, :, at:at + count],
                    is_down if side else is_up, is_up if side else is_down, down if side else up)
        if k == MAIN - 1:
            when(is_down, copies_m[0].wait_recv)
            when(is_up, copies_m[1].wait_recv)
            when(is_up2, copies_m[2].start)
            when(is_down2, copies_m[3].start)
            across_copy(across.at[1, :, 16:18], landed_far.at[1], is_down2, is_up2, down2)
            across_copy(across.at[0, :, 0:2], landed_far.at[0], is_up2, is_down2, up2)

    for one in loads:
        one.wait()
    for one in small[2:]:
        one.wait()
    for k in range(32):
        bias1[k:k + 1] = jnp.full((1, 128), b1[k], F32)
        bias2[k:k + 1] = jnp.full((1, 128), b2[k], F32)
    flat1[...] = jnp.zeros((64, 32), F32)
    for dr in range(3):
        for dc in range(3):
            for dz in range(3):
                at = ((dz * 3 + dr) * 3 + dc) * 2
                flat1[at:at + 2] = w1_in[dr, dc, dz].astype(F32)
    tap = lax.broadcasted_iota(jnp.int32, (64, 256), 0)
    lane = lax.broadcasted_iota(jnp.int32, (64, 256), 1)
    target = (tap // 18) * 80 + ((tap // 6) % 3) * 16 + (tap % 2) * 8 + (tap // 2) % 3
    spread = jnp.where((lane == target) & (tap < 54), 1.0, 0.0).astype(BF16)
    strip = lax.dot_general(flat1[...].astype(BF16), spread, (((0,), (0,)), ((), ())),
                            preferred_element_type=F32)
    for i, ocol in enumerate(COLUMNS):
        for orow in range(3):
            at = (i * 3 + orow) * 32
            band1[at:at + 32] = pltpu.roll(strip, orow * 16 + ocol, 1).astype(BF16)
    zero = jnp.zeros((32, 128), BF16)
    for dz in range(3):
        strips = []
        for dr in range(3):
            taps = jnp.concatenate(
                [w2_in[dr, dc, dz].astype(F32) for dc in range(3)] + [jnp.zeros((32, 32), F32)], axis=0)
            taps = jnp.concatenate([taps, jnp.zeros((128, 96), F32)], axis=1)
            flipped = taps.T[0:32]
            strips.append((flipped.astype(BF16), pltpu.roll(flipped, 32, 1).astype(BF16)))
        for orow in range(2):
            for ocol in range(2):
                at = (orow * 2 + ocol) * 32
                for irow in range(4):
                    dr = irow - orow
                    band2[at:at + 32, dz * 512 + irow * 128:dz * 512 + irow * 128 + 128] = (
                        strips[dr][ocol] if 0 <= dr < 3 else zero)
    hrow = lax.broadcasted_iota(jnp.int32, (32, 512), 0)
    hlane = lax.broadcasted_iota(jnp.int32, (32, 512), 1)
    feat = lax.broadcasted_iota(jnp.int32, (32, 512), 0)
    pick = jnp.where(feat == hlane % 32, 1.0, 0.0).astype(BF16)
    per_lane = jnp.dot(hw_in[...], pick, preferred_element_type=F32)
    cell_row = (hlane // 64) % 2
    cell_col = (hlane // 128) * 2 + (hlane // 32) % 2
    match = ((hrow // 8) % 2 == cell_row) & (hrow % 8 == cell_col)
    by_channel = jnp.where(hrow < 16, per_lane[0:1], per_lane[1:2])
    head[...] = jnp.where(match, by_channel, 0.0).astype(BF16)

    when(is_down2, copies_m[2].wait_recv)
    when(is_up2, copies_m[3].wait_recv)
    parts = ((0, 2, (-2, -1, 0)), (2, 8, (-1, 0, 1)), (10, 8, (-1, 0, 1)), (18, 2, (0, 1, 2)))
    for r0, count, reach in parts:
        weights = jnp.zeros((count, 16, 128), F32)
        for dp in reach:
            for j, dq in ((0, 0), (1, -1), (2, 1)):
                meta = metas_x[2 + dp, j]
                at = [meta[k:k + 1][None] for k in range(6)]
                rows = ramp(iota((count, 1, 128), 0) + (r0 - 2 - 16.0 * dp) - at[0], at[2], at[3])
                cols = ramp(iota((1, 16, 128), 1) - 16.0 * dq - at[1], at[4], at[5])
                weights = weights + rows * cols
        inverse[r0:r0 + count] = 1.0 / weights

    for k in range(FOLDED, len(CHUNKS)):
        when(is_right, copies_y[2 * k].wait_recv)
        when(is_left, copies_y[2 * k + 1].wait_recv)
    for r0, count, _ in parts:
        image[:, r0:r0 + count, 8:24] = row_sum(14 + r0, count)

    def fold(r0, count):
        total = image[:, r0:r0 + count, 8:24]
        if r0 < 18:
            total = total + decode(landed_x[1, :, r0:r0 + count], STEP_X)
        else:
            total = total + decode(landed_far[0], STEP_X)
        if r0 >= 2:
            total = total + decode(landed_x[0, :, r0 - 2:r0 - 2 + count], STEP_X)
        else:
            total = total + decode(landed_far[1], STEP_X)
        cells = total * inverse[r0:r0 + count][None]
        image[:, r0:r0 + count, 8:24] = cells
        return cells

    copies_h = [
        pltpu.make_async_remote_copy(
            image.at[:, r0:r0 + count, src:src + 2], image.at[:, r0:r0 + count, dst:dst + 2],
            send_h.at[2 * k + way], recv_h.at[2 * k + way],
            device_id=(p, there), device_id_type=MESH)
        for k, (r0, count) in enumerate(((2, 16), (0, 2), (18, 2)))
        for way, src, dst, there in ((0, 8, 24, left), (1, 22, 6, right))
    ]
    for k in range(MAIN):
        when(ways_x[k][1], copies_x[k].wait_recv)
    for r0 in (2, 10):
        joined[:, r0 - 2:r0 + 6] = fold(r0, 8)
    when(is_left, copies_h[0].start)
    when(is_right, copies_h[1].start)

    def stack(block, at, rows):
        cells = jnp.concatenate([image[ch, rows, c:c + 8 // len(at)] for ch in range(2) for c in at], axis=1)
        stack1[block, 1, rows] = cells.astype(BF16)
        stack1[block, 0, rows] = shift_planes(cells, 1).astype(BF16)
        stack1[block, 2, rows] = shift_planes(cells, -1).astype(BF16)

    def conv1(block, rows, low, high, places):
        halves = []
        for r0 in rows:
            parts = [stack1[block, dz, r0:r0 + 5].reshape(80, 128) for dz in range(3)]
            halves.append(jnp.concatenate(parts + [jnp.zeros((16, 128), BF16)], axis=0))
        count, lanes = (high - low) // 96, 128 * len(rows)
        bias = jnp.concatenate([bias1[...]] * len(rows), axis=1)
        out = jnp.dot(band1[low:high], jnp.concatenate(halves, axis=1), preferred_element_type=F32)
        out = jnp.maximum(out.reshape(3 * count, 32, lanes) + bias[None], 0.0).astype(BF16)
        for dz in range(3):
            one = out if dz == 1 else shift_planes(out, 1 - dz)
            one = one.reshape(count, 3, 32, lanes)
            for a, r0 in enumerate(rows):
                for i, place in enumerate(places):
                    first[dz, r0:r0 + 3, place] = one[i, :, :, a * 128:a * 128 + 128]

    def inner(rows):
        conv1(0, rows, 0, 576, [2 + c for c in COLUMNS])
        conv1(1, rows, 0, 576, [8 + c for c in COLUMNS])
        conv1(2, rows, 192, 384, [14, 15])

    blocks = ((0, (8,)), (1, (14,)), (2, (16,)))
    for block, at in blocks:
        stack(block, at, slice(2, 18))
    inner((3, 6))
    inner((9, 12))

    for one, way in zip(copies_x[MAIN:], ways_x[MAIN:]):
        when(way[1], one.wait_recv)
    fold(0, 2)
    fold(18, 2)

    @pl.when(p == 0)
    def _():
        image[:, 0:2, 8:24] = jnp.zeros((2, 2, 16, 128), F32)

    @pl.when(p == nx - 1)
    def _():
        image[:, 18:20, 8:24] = jnp.zeros((2, 2, 16, 128), F32)

    for k in (1, 2):
        when(is_left, copies_h[2 * k].start)
        when(is_right, copies_h[2 * k + 1].start)
    for block, at in blocks:
        stack(block, at, slice(0, 2))
        stack(block, at, slice(18, 20))
    inner((0, 15))

    def clear_rows(low, high):
        @pl.when(p == 0)
        def _():
            first[:, 0:1, low:high] = jnp.zeros((3, 1, high - low, 32, 128), BF16)

        @pl.when(p == nx - 1)
        def _():
            first[:, 17:18, low:high] = jnp.zeros((3, 1, high - low, 32, 128), BF16)

    clear_rows(2, 16)

    bias = jnp.concatenate([jnp.concatenate([bias2[...]] * 4, axis=0)] * 4, axis=1)

    def conv2(quad, blocks, slot, b0):
        cols = []
        for c0 in blocks:
            for a in range(2):
                r0 = quad * 4 + 2 * a
                cols.append(jnp.concatenate(
                    [first[dz, r0:r0 + 4, c0:c0 + 4].reshape(512, 128) for dz in range(3)], axis=0))
        out = jnp.dot(band2[...], jnp.concatenate(cols, axis=1), preferred_element_type=F32)
        out = jnp.maximum(out + bias, 0.0).astype(BF16)
        for j in range(2):
            second[(b0 + j) * 128:(b0 + j) * 128 + 128, slot * 256:slot * 256 + 256] = (
                out[:, j * 256:j * 256 + 256])

    def project(quad, slot, places):
        out = jnp.dot(head[...], second[:, slot * 256:slot * 256 + 256], preferred_element_type=F32)
        for ch in range(2):
            for a in range(2):
                for r in range(2):
                    cells = out[ch * 16 + r * 8:ch * 16 + r * 8 + 8, a * 128:a * 128 + 128] + hb[ch]
                    for src, dst, count in places:
                        restored[ch, quad * 4 + 2 * a + r, dst:dst + count, :] = cells[src:src + count]

    for quad in range(4):
        conv2(quad, (2, 4), quad, 0)
        conv2(quad, (6, 8), quad, 2)
        conv2(quad, (10, 12), 4 + quad, 0)
        if quad > 0:
            project(quad - 1, quad - 1, ((0, 2, 8),))

    for k in range(3):
        when(is_right, copies_h[2 * k].wait_recv)
        when(is_left, copies_h[2 * k + 1].wait_recv)
    stack(3, (6, 22), slice(0, 20))
    conv1(3, (0, 3, 6, 9, 12, 15), 0, 384, [0, 1, 16, 17])
    clear_rows(0, 18)

    @pl.when(q == 0)
    def _():
        first[:, :, 0:1] = jnp.zeros((3, 18, 1, 32, 128), BF16)

    @pl.when(q == ny - 1)
    def _():
        first[:, :, 17:18] = jnp.zeros((3, 18, 1, 32, 128), BF16)

    project(3, 3, ((0, 2, 8),))
    for quad in range(4):
        conv2(quad, (0, 14), 4 + quad, 2)
        if quad > 0:
            project(quad - 1, 3 + quad, ((0, 10, 4), (4, 0, 2), (6, 14, 2)))
    project(3, 7, ((0, 10, 4), (4, 0, 2), (6, 14, 2)))

    when(is_left, meta_copies[0].wait_send)
    when(is_right, meta_copies[1].wait_send)
    for k, one in enumerate(copies_y):
        when(is_right if k % 2 else is_left, one.wait_send)
    for one, way in zip(copies_m, (is_up, is_down, is_up2, is_down2)):
        when(way, one.wait_send)
    for one, way in zip(copies_x, ways_x):
        when(way[0], one.wait_send)
    for k in range(3):
        when(is_left, copies_h[2 * k].wait_send)
        when(is_right, copies_h[2 * k + 1].wait_send)


def shards(tiles, shifts, extents, w1, b1, w2, b2, hw, hb):
    nx, ny = lax.axis_size("gx"), lax.axis_size("gy")
    vmem = pl.BlockSpec(memory_space=pltpu.VMEM)
    hbm = pl.BlockSpec(memory_space=pl.ANY)

    def body(*refs):
        kernel(nx, ny, *refs)

    dma = pltpu.SemaphoreType.DMA
    made = pl.pallas_call(
        body,
        out_shape=[pltpu.VMEM((2, 16, 16, 128), F32)] * 2,
        in_specs=[hbm] * 9,
        out_specs=[vmem, vmem],
        scratch_shapes=[
            pltpu.VMEM((2, 56, 56, 128), F32),
            pltpu.VMEM((2, 2, 48, 16, 128), I16),
            pltpu.VMEM((2, 2, 48, 16, 128), I16),
            pltpu.VMEM((1, 8, 128), F32),
            pltpu.VMEM((5, 3, 8, 128), F32),
            pltpu.VMEM((2, 2, 18, 16, 128), I16),
            pltpu.VMEM((2, 2, 18, 16, 128), I16),
            pltpu.VMEM((2, 2, 2, 16, 128), I16),
            pltpu.VMEM((2, 20, 32, 128), F32),
            pltpu.VMEM((4, 3, 20, 16, 128), BF16),
            pltpu.VMEM((3, 18, 18, 32, 128), BF16),
            pltpu.VMEM((3, 3, 3, 2, 32), BF16),
            pltpu.VMEM((3, 3, 3, 32, 32), BF16),
            pltpu.VMEM((2, 32), BF16),
            pltpu.VMEM((576, 256), BF16),
            pltpu.VMEM((128, 1536), BF16),
            pltpu.VMEM((32, 512), BF16),
            pltpu.VMEM((32, 128), F32),
            pltpu.VMEM((32, 128), F32),
            pltpu.VMEM((64, 32), F32),
            pltpu.VMEM((512, 2048), BF16),
            pltpu.VMEM((20, 16, 128), F32),
            pltpu.SMEM((1, 1, 2), jnp.int32),
            pltpu.SMEM((1, 1, 4), jnp.int32),
            pltpu.SMEM((32,), F32),
            pltpu.SMEM((32,), F32),
            pltpu.SMEM((2,), F32),
            dma((5,)),
            dma((4,)), dma((2, len(CHUNKS))), dma((2, len(CHUNKS))), dma((FOLDED + 2,)), dma((FOLDED + 2,)), dma((6,)), dma((6,)), dma((6,)), dma((6,)),
        ],
        compiler_params=pltpu.CompilerParams(
            collective_id=0, has_side_effects=True, vmem_limit_bytes=60 * 1024 * 1024),
    )(tiles, shifts, extents, w1, b1, w2, b2, hw.T, hb)
    return pl.pallas_call(
        hand_over,
        out_shape=[jax.ShapeDtypeStruct((2, 16, 16, 128), F32)] * 2,
        in_specs=[vmem, vmem],
        out_specs=[hbm, hbm],
        scratch_shapes=[dma((4,))],
        compiler_params=pltpu.CompilerParams(vmem_limit_bytes=16 * 1024 * 1024),
    )(*made)


def hand_over(joined, restored, joined_out, restored_out, sem):
    copies = []
    for k, (src, dst) in enumerate(((joined, joined_out), (restored, restored_out))):
        for ch in range(2):
            one = pltpu.make_async_copy(src.at[ch], dst.at[ch], sem.at[2 * k + ch])
            one.start()
            copies.append(one)
    for one in copies:
        one.wait()


def solution(mesh):
    return jax.shard_map(
        shards,
        mesh=mesh,
        in_specs=(P("gx", "gy"), P("gx", "gy"), P("gx", "gy"), P(), P(), P(), P(), P(), P()),
        out_specs=(P(None, "gx", "gy", None), P(None, "gx", "gy", None)),
        check_vma=False,
    )
```

```python
import jax
import jax.numpy as jnp
from jax import lax
from jax.experimental import pallas as pl
from jax.experimental.pallas import tpu as pltpu
from jax.sharding import PartitionSpec as P

MESH = pl.DeviceIdType.MESH
F32 = jnp.float32
BF16 = jnp.bfloat16
I16 = jnp.int16
STEP_Y = 4.0 / 32767
STEP_X = 12.0 / 32767
PAD = 8
CHUNKS = ((32, 4), (0, 4), (36, 4), (4, 4), (40, 8), (8, 8), (30, 2), (16, 2), (18, 6), (24, 6))
FOLDED = 8
MAIN = 6
COLUMNS = (0, 1, 4, 5, 2, 3)


def ramp(places, before, after):
    rise = places + 1.0 + before
    fall = 16.0 + after - places
    return jnp.clip(jnp.minimum(rise, fall), 0.0, 8.0) * 0.125


def code(values, step):
    return (values * (1.0 / step) + 0.5).astype(jnp.int32).astype(I16)


def decode(values, step):
    return values.astype(jnp.int32).astype(F32) * step


def when(condition, action):
    pl.when(condition)(action)


def shift_planes(x, by):
    lane = lax.broadcasted_iota(jnp.int32, x.shape[:-1] + (128,), x.ndim - 1)
    parts = []
    for g in range(x.shape[-1] // 128):
        one = pltpu.roll(x[..., g * 128:g * 128 + 128], by % 128, x.ndim - 1)
        parts.append(jnp.where(lane == (0 if by > 0 else 127), jnp.zeros_like(one), one))
    return jnp.concatenate(parts, axis=-1)


def iota(shape, dim):
    return lax.broadcasted_iota(jnp.int32, shape, dim).astype(F32)


def kernel(
    nx, ny,
    tiles, shifts_in, extents_in, w1, b1_in, w2, b2_in, hw, hb_in,
    joined, restored,
    tile, sides, landed, metas, metas_x, across, landed_x, landed_far, image, stack1, first,
    w1_in, w2_in, hw_in, band1, band2, head, bias1, bias2, flat1, second, inverse, shifts, extents, b1, b2, hb, small_sem,
    in_sem, send_y, recv_y, send_x, recv_x, send_m, recv_m, send_h, recv_h,
):
    p, q = lax.axis_index("gx"), lax.axis_index("gy")
    up, down = lax.rem(p + nx - 1, nx), lax.rem(p + 1, nx)
    up2, down2 = lax.rem(p + nx - 2, nx), lax.rem(p + 2, nx)
    left, right = lax.rem(q + ny - 1, ny), lax.rem(q + 1, ny)

    barrier = pltpu.get_barrier_semaphore()
    is_up, is_down, is_left, is_right = p > 0, p < nx - 1, q > 0, q < ny - 1
    is_up2, is_down2 = p > 1, p < nx - 2
    near = ((is_left, (p, left)), (is_right, (p, right)), (is_up, (up, q)), (is_down, (down, q)))
    for there_is, there in near:
        @pl.when(there_is)
        def _():
            pl.semaphore_signal(barrier, inc=1, device_id=there, device_id_type=MESH)

    small = [
        pltpu.make_async_copy(src, dst, small_sem.at[k])
        for k, (src, dst) in enumerate(
            ((shifts_in, shifts), (extents_in, extents), (b1_in, b1), (b2_in, b2), (hb_in, hb)))
    ]
    for one in small:
        one.start()
    load = pltpu.make_async_copy(tiles.at[0, 0], tile.at[:, PAD:PAD + 40, PAD:PAD + 40], in_sem.at[0])
    load.start()
    loads = [
        pltpu.make_async_copy(w1, w1_in, in_sem.at[1]),
        pltpu.make_async_copy(w2, w2_in, in_sem.at[2]),
        pltpu.make_async_copy(hw, hw_in, in_sem.at[3]),
    ]
    for one in loads:
        one.start()
    @pl.when(q == 0)
    def _():
        landed[1] = jnp.zeros((2, 48, 16, 128), I16)
        metas_x[2, 1] = jnp.full((8, 128), -100.0, F32)
        image[:, :, 6:8] = jnp.zeros((2, 20, 2, 128), F32)

    @pl.when(q == ny - 1)
    def _():
        landed[0] = jnp.zeros((2, 48, 16, 128), I16)
        metas_x[2, 2] = jnp.full((8, 128), -100.0, F32)
        image[:, :, 24:26] = jnp.zeros((2, 20, 2, 128), F32)

    @pl.when(p == 0)
    def _():
        landed_x[1] = jnp.zeros((2, 18, 16, 128), I16)
        metas_x[1] = jnp.full((3, 8, 128), -100.0, F32)

    @pl.when(p == nx - 1)
    def _():
        landed_x[0] = jnp.zeros((2, 18, 16, 128), I16)
        metas_x[3] = jnp.full((3, 8, 128), -100.0, F32)

    @pl.when(p <= 1)
    def _():
        landed_far[1] = jnp.zeros((2, 2, 16, 128), I16)
        metas_x[0] = jnp.full((3, 8, 128), -100.0, F32)

    @pl.when(p >= nx - 2)
    def _():
        landed_far[0] = jnp.zeros((2, 2, 16, 128), I16)
        metas_x[4] = jnp.full((3, 8, 128), -100.0, F32)

    tile[:, 0:PAD] = jnp.zeros((2, PAD, 56, 128), F32)
    tile[:, 48:56] = jnp.zeros((2, PAD, 56, 128), F32)
    tile[:, PAD:48, 0:PAD] = jnp.zeros((2, 40, PAD, 128), F32)
    tile[:, PAD:48, 48:56] = jnp.zeros((2, 40, PAD, 128), F32)

    small[0].wait()
    small[1].wait()
    s0, s1 = shifts[0, 0, 0], shifts[0, 0, 1]
    values = [shifts[0, 0, 0], shifts[0, 0, 1]] + [extents[0, 0, k] for k in range(4)]
    values = [v.astype(F32) for v in values]
    s0f, s1f, m0, m1, m2, m3 = values
    for k in range(6):
        metas[0, k:k + 1] = jnp.full((1, 128), values[k], F32)

    near_count = sum(there_is.astype(jnp.int32) for there_is, _ in near)
    pl.semaphore_wait(barrier, near_count)
    meta_copies = [
        pltpu.make_async_remote_copy(metas.at[0], metas_x.at[2, 2], send_m.at[0], recv_m.at[0],
                                     device_id=(p, left), device_id_type=MESH),
        pltpu.make_async_remote_copy(metas.at[0], metas_x.at[2, 1], send_m.at[1], recv_m.at[1],
                                     device_id=(p, right), device_id_type=MESH),
    ]
    when(is_left, meta_copies[0].start)
    when(is_right, meta_copies[1].start)
    load.wait()

    def own(r0, count, c0, width_vec):
        rows = ramp(iota((count, 1, 128), 0) + (r0 - 16.0) - s0f, m0, m1)
        weight = rows * width_vec
        return tile[:, pl.ds(r0 + 4 - s0 , count), pl.ds(c0 + 4 - s1, 16), :] * weight[None]

    def row_sum(r0, count):
        total = own(r0, count, 16, col_mid)
        total = total + decode(landed[0, :, r0:r0 + count], STEP_Y)
        return total + decode(landed[1, :, r0:r0 + count], STEP_Y)

    def columns(c0):
        return ramp(iota((1, 16, 128), 1) + (c0 - 16.0) - s1f, m2, m3)

    col_left, col_mid, col_right = columns(0), columns(16), columns(32)
    copies_y = []
    for k, (r0, count) in enumerate(CHUNKS):
        for side, (c0, vec, there) in enumerate(((0, col_left, left), (32, col_right, right))):
            sides[side, :, r0:r0 + count] = code(own(r0, count, c0, vec), STEP_Y)
            one = pltpu.make_async_remote_copy(
                sides.at[side, :, r0:r0 + count], landed.at[side, :, r0:r0 + count],
                send_y.at[side, k], recv_y.at[side, k], device_id=(p, there), device_id_type=MESH)
            when(is_right if side else is_left, one.start)
            copies_y.append(one)

    when(is_right, meta_copies[0].wait_recv)
    when(is_left, meta_copies[1].wait_recv)
    metas_x[2, 0] = metas[0]
    copies_m = [
        pltpu.make_async_remote_copy(metas_x.at[2], metas_x.at[2 + by], send_m.at[k], recv_m.at[k],
                                     device_id=(there, q), device_id_type=MESH)
        for k, by, there in ((2, 1, up), (3, -1, down), (4, 2, up2), (5, -2, down2))
    ]
    when(is_up, copies_m[0].start)
    when(is_down, copies_m[1].start)

    copies_x, ways_x = [], []

    def across_copy(src, dst, out, back, there):
        k = len(copies_x)
        one = pltpu.make_async_remote_copy(src, dst, send_x.at[k], recv_x.at[k],
                                           device_id=(there, q), device_id_type=MESH)
        when(out, one.start)
        copies_x.append(one)
        ways_x.append((out, back))

    for k in range(FOLDED):
        r0, count = CHUNKS[k]
        when(is_right, copies_y[2 * k].wait_recv)
        when(is_left, copies_y[2 * k + 1].wait_recv)
        side = 1 if r0 >= 30 else 0
        at = r0 - 30 * side
        across[side, :, at:at + count] = code(row_sum(r0, count), STEP_X)
        across_copy(across.at[side, :, at:at + count], landed_x.at[side, :, at:at + count],
                    is_down if side else is_up, is_up if side else is_down, down if side else up)
        if k == MAIN - 1:
            when(is_down, copies_m[0].wait_recv)
            when(is_up, copies_m[1].wait_recv)
            when(is_up2, copies_m[2].start)
            when(is_down2, copies_m[3].start)
            across_copy(across.at[1, :, 16:18], landed_far.at[1], is_down2, is_up2, down2)
            across_copy(across.at[0, :, 0:2], landed_far.at[0], is_up2, is_down2, up2)

    for one in loads:
        one.wait()
    for one in small[2:]:
        one.wait()
    for k in range(32):
        bias1[k:k + 1] = jnp.full((1, 128), b1[k], F32)
        bias2[k:k + 1] = jnp.full((1, 128), b2[k], F32)
    flat1[...] = jnp.zeros((64, 32), F32)
    for dr in range(3):
        for dc in range(3):
            for dz in range(3):
                at = ((dz * 3 + dr) * 3 + dc) * 2
                flat1[at:at + 2] = w1_in[dr, dc, dz].astype(F32)
    tap = lax.broadcasted_iota(jnp.int32, (64, 256), 0)
    lane = lax.broadcasted_iota(jnp.int32, (64, 256), 1)
    target = (tap // 18) * 80 + ((tap // 6) % 3) * 16 + (tap % 2) * 8 + (tap // 2) % 3
    spread = jnp.where((lane == target) & (tap < 54), 1.0, 0.0).astype(BF16)
    strip = lax.dot_general(flat1[...].astype(BF16), spread, (((0,), (0,)), ((), ())),
                            preferred_element_type=F32)
    for i, ocol in enumerate(COLUMNS):
        for orow in range(3):
            at = (i * 3 + orow) * 32
            band1[at:at + 32] = pltpu.roll(strip, orow * 16 + ocol, 1).astype(BF16)
    zero = jnp.zeros((32, 128), BF16)
    for dz in range(3):
        strips = []
        for dr in range(3):
            taps = jnp.concatenate(
                [w2_in[dr, dc, dz].astype(F32) for dc in range(3)] + [jnp.zeros((32, 32), F32)], axis=0)
            taps = jnp.concatenate([taps, jnp.zeros((128, 96), F32)], axis=1)
            flipped = taps.T[0:32]
            strips.append((flipped.astype(BF16), pltpu.roll(flipped, 32, 1).astype(BF16)))
        for orow in range(2):
            for ocol in range(2):
                at = (orow * 2 + ocol) * 32
                for irow in range(4):
                    dr = irow - orow
                    band2[at:at + 32, dz * 512 + irow * 128:dz * 512 + irow * 128 + 128] = (
                        strips[dr][ocol] if 0 <= dr < 3 else zero)
    hrow = lax.broadcasted_iota(jnp.int32, (32, 512), 0)
    hlane = lax.broadcasted_iota(jnp.int32, (32, 512), 1)
    feat = lax.broadcasted_iota(jnp.int32, (32, 512), 0)
    pick = jnp.where(feat == hlane % 32, 1.0, 0.0).astype(BF16)
    per_lane = jnp.dot(hw_in[...], pick, preferred_element_type=F32)
    cell_row = (hlane // 64) % 2
    cell_col = (hlane // 128) * 2 + (hlane // 32) % 2
    match = ((hrow // 8) % 2 == cell_row) & (hrow % 8 == cell_col)
    by_channel = jnp.where(hrow < 16, per_lane[0:1], per_lane[1:2])
    head[...] = jnp.where(match, by_channel, 0.0).astype(BF16)

    when(is_down2, copies_m[2].wait_recv)
    when(is_up2, copies_m[3].wait_recv)
    parts = ((0, 2, (-2, -1, 0)), (2, 8, (-1, 0, 1)), (10, 8, (-1, 0, 1)), (18, 2, (0, 1, 2)))
    for r0, count, reach in parts:
        weights = jnp.zeros((count, 16, 128), F32)
        for dp in reach:
            for j, dq in ((0, 0), (1, -1), (2, 1)):
                meta = metas_x[2 + dp, j]
                at = [meta[k:k + 1][None] for k in range(6)]
                rows = ramp(iota((count, 1, 128), 0) + (r0 - 2 - 16.0 * dp) - at[0], at[2], at[3])
                cols = ramp(iota((1, 16, 128), 1) - 16.0 * dq - at[1], at[4], at[5])
                weights = weights + rows * cols
        inverse[r0:r0 + count] = 1.0 / weights

    for k in range(FOLDED, len(CHUNKS)):
        when(is_right, copies_y[2 * k].wait_recv)
        when(is_left, copies_y[2 * k + 1].wait_recv)
    for r0, count, _ in parts:
        image[:, r0:r0 + count, 8:24] = row_sum(14 + r0, count)

    def fold(r0, count):
        total = image[:, r0:r0 + count, 8:24]
        if r0 < 18:
            total = total + decode(landed_x[1, :, r0:r0 + count], STEP_X)
        else:
            total = total + decode(landed_far[0], STEP_X)
        if r0 >= 2:
            total = total + decode(landed_x[0, :, r0 - 2:r0 - 2 + count], STEP_X)
        else:
            total = total + decode(landed_far[1], STEP_X)
        cells = total * inverse[r0:r0 + count][None]
        image[:, r0:r0 + count, 8:24] = cells
        return cells

    copies_h = [
        pltpu.make_async_remote_copy(
            image.at[:, r0:r0 + count, src:src + 2], image.at[:, r0:r0 + count, dst:dst + 2],
            send_h.at[2 * k + way], recv_h.at[2 * k + way],
            device_id=(p, there), device_id_type=MESH)
        for k, (r0, count) in enumerate(((2, 16), (0, 2), (18, 2)))
        for way, src, dst, there in ((0, 8, 24, left), (1, 22, 6, right))
    ]
    for k in range(MAIN):
        when(ways_x[k][1], copies_x[k].wait_recv)
    for r0 in (2, 10):
        joined[:, r0 - 2:r0 + 6] = fold(r0, 8)
    when(is_left, copies_h[0].start)
    when(is_right, copies_h[1].start)

    def stack(block, at, rows):
        cells = jnp.concatenate([image[ch, rows, c:c + 8 // len(at)] for ch in range(2) for c in at], axis=1)
        stack1[block, 1, rows] = cells.astype(BF16)
        stack1[block, 0, rows] = shift_planes(cells, 1).astype(BF16)
        stack1[block, 2, rows] = shift_planes(cells, -1).astype(BF16)

    def conv1(block, rows, low, high, places):
        halves = []
        for r0 in rows:
            parts = [stack1[block, dz, r0:r0 + 5].reshape(80, 128) for dz in range(3)]
            halves.append(jnp.concatenate(parts + [jnp.zeros((16, 128), BF16)], axis=0))
        count, lanes = (high - low) // 96, 128 * len(rows)
        bias = jnp.concatenate([bias1[...]] * len(rows), axis=1)
        out = jnp.dot(band1[low:high], jnp.concatenate(halves, axis=1), preferred_element_type=F32)
        out = jnp.maximum(out.reshape(3 * count, 32, lanes) + bias[None], 0.0).astype(BF16)
        for dz in range(3):
            one = out if dz == 1 else shift_planes(out, 1 - dz)
            one = one.reshape(count, 3, 32, lanes)
            for a, r0 in enumerate(rows):
                for i, place in enumerate(places):
                    first[dz, r0:r0 + 3, place] = one[i, :, :, a * 128:a * 128 + 128]

    def inner(rows):
        conv1(0, rows, 0, 576, [2 + c for c in COLUMNS])
        conv1(1, rows, 0, 576, [8 + c for c in COLUMNS])
        conv1(2, rows, 192, 384, [14, 15])

    blocks = ((0, (8,)), (1, (14,)), (2, (16,)))
    for block, at in blocks:
        stack(block, at, slice(2, 18))
    inner((3, 6))
    inner((9, 12))

    for one, way in zip(copies_x[MAIN:], ways_x[MAIN:]):
        when(way[1], one.wait_recv)
    fold(0, 2)
    fold(18, 2)

    @pl.when(p == 0)
    def _():
        image[:, 0:2, 8:24] = jnp.zeros((2, 2, 16, 128), F32)

    @pl.when(p == nx - 1)
    def _():
        image[:, 18:20, 8:24] = jnp.zeros((2, 2, 16, 128), F32)

    for k in (1, 2):
        when(is_left, copies_h[2 * k].start)
        when(is_right, copies_h[2 * k + 1].start)
    for block, at in blocks:
        stack(block, at, slice(0, 2))
        stack(block, at, slice(18, 20))
    inner((0, 15))

    def clear_rows(low, high):
        @pl.when(p == 0)
        def _():
            first[:, 0:1, low:high] = jnp.zeros((3, 1, high - low, 32, 128), BF16)

        @pl.when(p == nx - 1)
        def _():
            first[:, 17:18, low:high] = jnp.zeros((3, 1, high - low, 32, 128), BF16)

    clear_rows(2, 16)

    bias = jnp.concatenate([jnp.concatenate([bias2[...]] * 4, axis=0)] * 4, axis=1)

    def conv2(quad, blocks, slot, b0):
        cols = []
        for c0 in blocks:
            for a in range(2):
                r0 = quad * 4 + 2 * a
                cols.append(jnp.concatenate(
                    [first[dz, r0:r0 + 4, c0:c0 + 4].reshape(512, 128) for dz in range(3)], axis=0))
        out = jnp.dot(band2[...], jnp.concatenate(cols, axis=1), preferred_element_type=F32)
        out = jnp.maximum(out + bias, 0.0).astype(BF16)
        for j in range(2):
            second[(b0 + j) * 128:(b0 + j) * 128 + 128, slot * 256:slot * 256 + 256] = (
                out[:, j * 256:j * 256 + 256])

    def project(quad, slot, places):
        out = jnp.dot(head[...], second[:, slot * 256:slot * 256 + 256], preferred_element_type=F32)
        for ch in range(2):
            for a in range(2):
                for r in range(2):
                    cells = out[ch * 16 + r * 8:ch * 16 + r * 8 + 8, a * 128:a * 128 + 128] + hb[ch]
                    for src, dst, count in places:
                        restored[ch, quad * 4 + 2 * a + r, dst:dst + count, :] = cells[src:src + count]

    for quad in range(4):
        conv2(quad, (2, 4), quad, 0)
        conv2(quad, (6, 8), quad, 2)
        conv2(quad, (10, 12), 4 + quad, 0)
        if quad > 0:
            project(quad - 1, quad - 1, ((0, 2, 8),))

    for k in range(3):
        when(is_right, copies_h[2 * k].wait_recv)
        when(is_left, copies_h[2 * k + 1].wait_recv)
    stack(3, (6, 22), slice(0, 20))
    conv1(3, (0, 3, 6, 9, 12, 15), 0, 384, [0, 1, 16, 17])
    clear_rows(0, 18)

    @pl.when(q == 0)
    def _():
        first[:, :, 0:1] = jnp.zeros((3, 18, 1, 32, 128), BF16)

    @pl.when(q == ny - 1)
    def _():
        first[:, :, 17:18] = jnp.zeros((3, 18, 1, 32, 128), BF16)

    project(3, 3, ((0, 2, 8),))
    for quad in range(4):
        conv2(quad, (0, 14), 4 + quad, 2)
        if quad > 0:
            project(quad - 1, 3 + quad, ((0, 10, 4), (4, 0, 2), (6, 14, 2)))
    project(3, 7, ((0, 10, 4), (4, 0, 2), (6, 14, 2)))

    when(is_left, meta_copies[0].wait_send)
    when(is_right, meta_copies[1].wait_send)
    for k, one in enumerate(copies_y):
        when(is_right if k % 2 else is_left, one.wait_send)
    for one, way in zip(copies_m, (is_up, is_down, is_up2, is_down2)):
        when(way, one.wait_send)
    for one, way in zip(copies_x, ways_x):
        when(way[0], one.wait_send)
    for k in range(3):
        when(is_left, copies_h[2 * k].wait_send)
        when(is_right, copies_h[2 * k + 1].wait_send)


def shards(tiles, shifts, extents, w1, b1, w2, b2, hw, hb):
    nx, ny = lax.axis_size("gx"), lax.axis_size("gy")
    vmem = pl.BlockSpec(memory_space=pltpu.VMEM)
    hbm = pl.BlockSpec(memory_space=pl.ANY)

    def body(*refs):
        kernel(nx, ny, *refs)

    dma = pltpu.SemaphoreType.DMA
    made = pl.pallas_call(
        body,
        out_shape=[pltpu.VMEM((2, 16, 16, 128), F32)] * 2,
        in_specs=[hbm] * 9,
        out_specs=[vmem, vmem],
        scratch_shapes=[
            pltpu.VMEM((2, 56, 56, 128), F32),
            pltpu.VMEM((2, 2, 48, 16, 128), I16),
            pltpu.VMEM((2, 2, 48, 16, 128), I16),
            pltpu.VMEM((1, 8, 128), F32),
            pltpu.VMEM((5, 3, 8, 128), F32),
            pltpu.VMEM((2, 2, 18, 16, 128), I16),
            pltpu.VMEM((2, 2, 18, 16, 128), I16),
            pltpu.VMEM((2, 2, 2, 16, 128), I16),
            pltpu.VMEM((2, 20, 32, 128), F32),
            pltpu.VMEM((4, 3, 20, 16, 128), BF16),
            pltpu.VMEM((3, 18, 18, 32, 128), BF16),
            pltpu.VMEM((3, 3, 3, 2, 32), BF16),
            pltpu.VMEM((3, 3, 3, 32, 32), BF16),
            pltpu.VMEM((2, 32), BF16),
            pltpu.VMEM((576, 256), BF16),
            pltpu.VMEM((128, 1536), BF16),
            pltpu.VMEM((32, 512), BF16),
            pltpu.VMEM((32, 128), F32),
            pltpu.VMEM((32, 128), F32),
            pltpu.VMEM((64, 32), F32),
            pltpu.VMEM((512, 2048), BF16),
            pltpu.VMEM((20, 16, 128), F32),
            pltpu.SMEM((1, 1, 2), jnp.int32),
            pltpu.SMEM((1, 1, 4), jnp.int32),
            pltpu.SMEM((32,), F32),
            pltpu.SMEM((32,), F32),
            pltpu.SMEM((2,), F32),
            dma((5,)),
            dma((4,)), dma((2, len(CHUNKS))), dma((2, len(CHUNKS))), dma((FOLDED + 2,)), dma((FOLDED + 2,)), dma((6,)), dma((6,)), dma((6,)), dma((6,)),
        ],
        compiler_params=pltpu.CompilerParams(
            collective_id=0, has_side_effects=True, vmem_limit_bytes=60 * 1024 * 1024),
    )(tiles, shifts, extents, w1, b1, w2, b2, hw.T, hb)
    return pl.pallas_call(
        hand_over,
        out_shape=[jax.ShapeDtypeStruct((2, 16, 16, 128), F32)] * 2,
        in_specs=[vmem, vmem],
        out_specs=[hbm, hbm],
        scratch_shapes=[dma((4,))],
        compiler_params=pltpu.CompilerParams(vmem_limit_bytes=16 * 1024 * 1024),
    )(*made)


def hand_over(joined, restored, joined_out, restored_out, sem):
    copies = []
    for k, (src, dst) in enumerate(((joined, joined_out), (restored, restored_out))):
        for ch in range(2):
            one = pltpu.make_async_copy(src.at[ch], dst.at[ch], sem.at[2 * k + ch])
            one.start()
            copies.append(one)
    for one in copies:
        one.wait()


def solution(mesh):
    return jax.shard_map(
        shards,
        mesh=mesh,
        in_specs=(P("gx", "gy"), P("gx", "gy"), P("gx", "gy"), P(), P(), P(), P(), P(), P()),
        out_specs=(P(None, "gx", "gy", None), P(None, "gx", "gy", None)),
        check_vma=False,
    )
```
